512 devices in a mesh: dp: 32 (over z, y_hi), tensor: 16 (over x, y_lo, core).
Axes of the slice: x: 4, y: 8 (y_hi: 4, y_lo: 2; y = y_hi * 2 + y_lo), z: 8, core: 2. Of those that a mesh axis runs over, the one named last changes fastest.
Arguments:
- teacher_in: bfloat16 [16384, 4096], P('dp', 'tensor'), may hold values from -6 to 6
- out_proj: bfloat16 [4096, 4096], P('tensor', 'dp'), may hold values from -0.09375 to 0.09375
- final_gain: float32 [4096], replicated, may hold values from 0.5 to 1.5
- mean_prev: float32 [4096], replicated, may hold values from -2 to 2
- rotation: bfloat16 [4096, 4096], P(None, 'tensor'), may hold values from -0.09375 to 0.09375
- signs: int32 [4096], P('tensor'), may hold values from 0 to 1
- prev_scale: float32 [1], replicated, may hold values from 0.5 to 2
- student_in: bfloat16 [16384, 1024], P('dp'), may hold values from -6 to 6
- head_weight: bfloat16 [1024, 4096], P(None, 'tensor'), may hold values from -0.1875 to 0.1875
- image_ids: int32 [16384], replicated, may hold values from 0 to 127, never falling along the last dimension, each value on 1 to 256 neighbouring positions
Outputs:
- new_cov: float32 [4096, 4096], P('tensor', 'dp')
- new_mean: float32 [4096], P('tensor')
- grad_head: float32 [1024, 4096], P(None, 'tensor')
- feature_loss: float32 [4096], P('tensor')
The draws below stay inside these ranges and needn't reach their ends.
Inputs may be any that keep to these rules, and one draw needn't show every extreme that they name: `image_ids`: image numbers never fall along the tokens; every image has at least one token and at most 256 tokens, some image has exactly that many when 16384 allows.
All inputs are finite; a program needn't handle non-finite values.
Results may differ from the reference program's by a relative error of at most 0.007.
Values may be sent and summed in bfloat16 or wider, within the bound.
No kernel may reach another device: no remote copies, remote signals or barrier semaphores. Data moves between devices by JAX's collectives and lax.ppermute only.
A program may use at most 128 MiB of HBM per device.

```python
import math
import jax
import jax.numpy as jnp
import numpy as np
from jax import lax

D = 4096
DS = 1024
TOKENS = 16384
IMAGES = 128
N_TENSOR = 16


def set_ends(result, stream_key, least, high):
    spot = [jax.random.randint(jax.random.fold_in(stream_key, axis), (), 0, length) for axis, length in enumerate(result.shape)]
    longest = result.shape.index(max(result.shape))
    neighbour = spot[:longest] + [(spot[longest] + 1) % result.shape[longest]] + spot[longest + 1:]
    return result.at[tuple(spot)].set(least).at[tuple(neighbour)].set(high)


def shard_levels(key, extent, shards, low, largest):
    loudness = 1.0
    for position, shards_of in shards:
        draws = jax.random.uniform(jax.random.fold_in(jax.random.fold_in(key, 6), position), (shards_of,), jnp.float32, low / len(shards), largest / len(shards))
        loudness = loudness * jnp.repeat(jnp.exp(draws), extent[position] // shards_of).reshape((-1,) + (1,) * (len(extent) - 1 - position))
    return loudness


def profile(number_of, total, most, lean):
    weights = [(1 << 20) // math.isqrt(standing ** lean) + 1 for standing in range(2, number_of + 1)]
    spare, holding = total - most - (number_of - 1), [1] * (number_of - 1)
    while spare > 0:
        candidates = [i for i in range(number_of - 1) if holding[i] < most]
        whole, left = sum([weights[i] for i in candidates]), spare
        for i in candidates:
            more = min(most - holding[i], max(1, left * weights[i] // whole), spare)
            holding[i] = holding[i] + more
            spare = spare - more
    return np.array([most] + holding)


def ragged_sizes(key, count, total, most, slope):
    if count == 2:
        one = jax.random.randint(key, (), max(1, total - most), min(most, total - 1) + 1)
        return jnp.stack([one, total - one])
    lengths = jnp.asarray(profile(count, total, most, slope), jnp.int32)
    couples = (count - 1) // 2
    giver, sink = lengths[1:1 + 2 * couples:2], lengths[2:2 + 2 * couples:2]
    slack = jnp.minimum(giver - 1, most - sink)
    moved = jax.random.randint(jax.random.fold_in(key, 1), (couples,), 0, 1 << 20) % (slack + 1)
    lengths = lengths.at[1:1 + 2 * couples:2].set(giver - moved).at[2:2 + 2 * couples:2].set(sink + moved)
    return lengths[jax.random.permutation(jax.random.fold_in(key, 2), count)]


def scatter_about(own_key, shape, scale, limit, pieces=(), kind=jnp.bfloat16):
    factor_of = shard_levels(own_key, shape, pieces, -0.22, 0.18) if pieces else 1.0
    drawn = jax.random.normal(own_key, shape, jnp.float32) * scale * factor_of
    return jnp.minimum(jnp.maximum(drawn, -limit), limit).astype(kind)


def setup_inputs(seed: int = 0) -> dict:
    keys = jax.random.split(jax.random.key(seed), 11)
    teacher_in = scatter_about(keys[0], (TOKENS, D), 1.0, 6.0, ((0, 32), (1, 16)))
    out_proj = scatter_about(keys[1], (D, D), D ** -0.5, 0.09375, ((0, 16), (1, 32)))
    final_gain = jnp.clip(1.0 + 0.1 * jax.random.normal(keys[2], (D,), jnp.float32), 0.5, 1.5)
    mean_prev = scatter_about(keys[3], (D,), 0.3, 2.0, (), jnp.float32)
    rotation = scatter_about(keys[4], (D, D), D ** -0.5, 0.09375, ((1, 16),))
    signs = set_ends(jax.random.randint(keys[5], (D,), 0, 2), jax.random.fold_in(keys[5], 1), 0, 1).astype(jnp.int32)
    prev_scale = jnp.clip(jnp.exp(jax.random.uniform(keys[6], (1,), jnp.float32, math.log(0.5), math.log(2.0))), 0.5, 2.0)
    student_in = scatter_about(keys[7], (TOKENS, DS), 1.0, 6.0, ((0, 32),))
    head_weight = scatter_about(keys[8], (DS, D), DS ** -0.5, 0.1875, ((1, 16),))
    image_ids = jnp.searchsorted(jnp.cumsum(ragged_sizes(keys[9], IMAGES, TOKENS, min(256, TOKENS - IMAGES + 1), 2)), jnp.arange(TOKENS), side="right").astype(jnp.int32)
    return {"teacher_in": teacher_in, "out_proj": out_proj, "final_gain": final_gain, "mean_prev": mean_prev, "rotation": rotation, "signs": signs, "prev_scale": prev_scale, "student_in": student_in, "head_weight": head_weight, "image_ids": image_ids}


def parity_sign(value):
    count = jnp.zeros_like(value)
    for place in range(16):
        count = count + (value >> place & 1)
    return 1 - 2 * (count % 2)

def hadamard(size):
    index = jnp.arange(size, dtype=jnp.int32)
    return parity_sign(index[:, None] & index[None, :]).astype(jnp.float32)

def layer_norm(values):
    centred = values - lax.optimization_barrier(jnp.mean(values, axis=-1, keepdims=True))
    spread = lax.optimization_barrier(jnp.mean(centred * centred, axis=-1, keepdims=True))
    return centred * lax.rsqrt(spread + 1e-06)

def reference(teacher_in, out_proj, final_gain, mean_prev, rotation, signs, prev_scale, student_in, head_weight, image_ids):
    block = D // N_TENSOR
    summed = jnp.dot(teacher_in, out_proj, preferred_element_type=jnp.float32)
    features = (layer_norm(summed) * final_gain).astype(jnp.bfloat16)
    moment = jnp.dot(features.T, features, preferred_element_type=jnp.float32)
    new_mean = lax.optimization_barrier(jnp.sum(features, axis=0, dtype=jnp.float32)) / TOKENS
    new_cov = moment / TOKENS - new_mean[:, None] * new_mean[None, :]
    shifted = (features.astype(jnp.float32) - mean_prev).astype(jnp.bfloat16)
    basis = jnp.dot(shifted, rotation, preferred_element_type=jnp.float32).astype(jnp.bfloat16)
    signed = basis.astype(jnp.float32) * (2 * signs - 1).astype(jnp.float32)
    stacked = signed.reshape(TOKENS, N_TENSOR, block)
    mixed = jnp.einsum('tbj,jk->tbk', stacked, hadamard(block), precision=lax.Precision.HIGHEST)
    rotated = jnp.einsum('tbk,cb->tck', mixed, hadamard(N_TENSOR), precision=lax.Precision.HIGHEST).reshape(TOKENS, D)
    target = rotated / (jnp.sqrt(jnp.float32(D)) * prev_scale[0])
    normed = layer_norm(student_in.astype(jnp.float32)).astype(jnp.bfloat16)
    predicted = jnp.dot(normed, head_weight, preferred_element_type=jnp.float32)
    residual = predicted - target
    image_nums = jnp.arange(IMAGES, dtype=jnp.int32)
    counts = lax.optimization_barrier(jnp.sum((image_ids[None, :] == image_nums[:, None]).astype(jnp.float32), axis=1))
    weight = 1.0 / counts[image_ids]
    feature_loss = lax.optimization_barrier(jnp.sum(weight[:, None] * residual * residual, axis=0)) / IMAGES
    scaled = (residual * weight[:, None]).astype(jnp.bfloat16)
    grad_head = jnp.dot(normed.T, scaled, preferred_element_type=jnp.float32)
    return (new_cov, new_mean, grad_head, feature_loss)
```

```python
import jax
import jax.numpy as jnp
from jax import lax
from jax.experimental import pallas as pl
from jax.experimental.pallas import tpu as pltpu
from jax.sharding import Mesh
from jax.sharding import PartitionSpec as P

DP = ("z", "yh")
TN = ("x", "yl", "c")
IMAGE_SHARE = 128
BF = jnp.bfloat16
F32 = jnp.float32


def hold(value):
    return lax.reduce_precision(value, 8, 7)


def split3(value):
    high = hold(value)
    rest = value - high
    mid = hold(rest)
    return high, mid, rest - mid


def shift(block, axis, step):
    count = lax.axis_size(axis)
    return lax.ppermute(block, axis, [(i, (i + step) % count) for i in range(count)])


def absolute(relative, axis):
    count = len(relative)
    twice = jnp.stack(relative + relative)
    return lax.dynamic_slice_in_dim(twice, count - lax.axis_index(axis), count, 0)


def gather_direct(block, axis):
    count = lax.axis_size(axis)
    return absolute([block] + [shift(block, axis, count - j) for j in range(1, count)], axis)


def gather_ring(block, axis):
    count = lax.axis_size(axis)
    ahead, behind = [block], [block]
    for _ in range(count // 2 - 1):
        ahead.append(shift(ahead[-1], axis, -1))
        behind.append(shift(behind[-1], axis, 1))
    half = block.shape[0] // 2
    far = jnp.concatenate([shift(ahead[-1][:half], axis, -1), shift(behind[-1][half:], axis, 1)])
    return absolute(ahead + [far] + behind[:0:-1], axis)


def gather_dp(block):
    near = gather_direct(block, "yh")
    near = near.reshape((-1,) + block.shape[1:])
    whole = gather_ring(near, "z")
    return whole.reshape((-1,) + block.shape[1:])


def parity_sign(value):
    count = jnp.zeros_like(value)
    for place in range(16):
        count = count + (value >> place & 1)
    return 1 - 2 * (count % 2)


def layer_norm(values):
    centred = values - jnp.mean(values, axis=-1, keepdims=True)
    spread = jnp.mean(centred * centred, axis=-1, keepdims=True)
    return centred * lax.rsqrt(spread + 1e-06)


def project_kernel(x_ref, w_ref, out_ref, stat_ref):
    own = w_ref.shape[1]
    total = jnp.zeros(out_ref.shape, F32)
    for b in range(x_ref.shape[0]):
        total += jnp.dot(x_ref[b], w_ref[b * own : (b + 1) * own, :], preferred_element_type=F32)
    mean = jnp.sum(total, axis=1, keepdims=True) * (1.0 / own)
    centred = total - mean
    out_ref[...] = centred.astype(BF)
    spread = jnp.sum(centred * centred, axis=1, keepdims=True)
    lane = lax.broadcasted_iota(jnp.int32, stat_ref.shape, 1)
    stat_ref[...] = jnp.where(lane == 0, mean, spread)


def main_kernel(
    pos_ref, scale_ref, g_ref, adj_ref, rstd_ref, gain_ref, prev_ref, rot_ref, pred_ref, w_ref, normed_ref,
    out_ref, f_ref,
):
    blocks, rows, own = f_ref.shape
    chunks = out_ref.shape[0]
    part = out_ref.shape[2]
    depth = normed_ref.shape[1] // chunks
    rstd = rstd_ref[...]
    total = jnp.zeros((rows, own), F32)
    sums = []
    for b in range(blocks):
        value = (g_ref[b, :rows, :].astype(F32) + adj_ref[:, b : b + 1]) * rstd * gain_ref[b]
        feature = value.astype(BF)
        f_ref[b] = feature
        feature = feature.astype(F32)
        sums.append(jnp.sum(feature, axis=0, keepdims=True))
        shifted = (feature - prev_ref[b]).astype(BF)
        total += jnp.dot(shifted, rot_ref[b * own : (b + 1) * own, :], preferred_element_type=F32)
    residual = pred_ref[...] - total * scale_ref[0]
    weighted = residual * w_ref[...]
    loss = jnp.sum(weighted * residual, axis=0, keepdims=True)
    grad = lax.dot_general(
        normed_ref[...], weighted.astype(BF), (((0,), (0,)), ((), ())), preferred_element_type=F32
    ).astype(BF)
    own_t = f_ref[pos_ref[0]].astype(F32).T
    own_col = jnp.sum(own_t, axis=1, keepdims=True)
    own_row = jnp.sum(f_ref[pos_ref[0]].astype(F32), axis=0, keepdims=True)
    own_t = own_t.astype(BF)
    for b in range(blocks):
        block = jnp.dot(own_t, f_ref[b], preferred_element_type=F32) - own_col * (sums[b] * (1.0 / rows))
        block = block.astype(BF)
        for h in range(2):
            out_ref[2 * b + h, :own, :] = block[:, h * part : (h + 1) * part]
    row = lax.broadcasted_iota(jnp.int32, (16, part), 0)

    def parts(value):
        high = value.astype(BF).astype(F32)
        rest = value - high
        mid = rest.astype(BF).astype(F32)
        return [high, mid, rest - mid]

    fixed = []
    for h in range(2):
        fixed += parts(own_row[:, h * part : (h + 1) * part])
    for h in range(2):
        fixed += parts(loss[:, h * part : (h + 1) * part])
    for d in range(chunks):
        for h in range(2):
            out_ref[d, own + h * depth : own + (h + 1) * depth, :] = grad[
                d * depth : (d + 1) * depth, h * part : (h + 1) * part
            ]
        tile = jnp.zeros((16, part), F32)
        here = sums[d // 2][:, (d % 2) * part : (d % 2 + 1) * part]
        for i, piece in enumerate(fixed + parts(here)):
            tile = jnp.where(row == i, piece, tile)
        out_ref[d, own + 2 * depth :, :] = tile.astype(BF)


def body(
    teacher_in,
    out_proj,
    final_gain,
    mean_prev,
    rotation,
    signs,
    prev_scale,
    student_in,
    head_weight,
    image_ids,
):
    rows, own = teacher_in.shape
    part = out_proj.shape[1]
    width = final_gain.shape[0]
    blocks = width // own
    chunks = width // part
    depth = student_in.shape[1] // chunks
    all_tokens = image_ids.shape[0]
    image_count = all_tokens // IMAGE_SHARE
    dpos = lax.axis_index(DP)
    tpos = lax.axis_index(TN)

    side = dpos % 2
    halves = out_proj.reshape(2, part, part)
    got = []
    for k in range(2):
        send = lax.dynamic_index_in_dim(halves, (side + k) % 2, 0, keepdims=False)
        route = []
        for d in range(chunks):
            for t in range(blocks):
                route.append((d * blocks + t, (2 * t + (d % 2 ^ k)) * blocks + d // 2))
        got.append(lax.ppermute(send, DP + TN, route))
    strip = jnp.where(
        side == 0, jnp.concatenate(got, axis=1), jnp.concatenate(got[::-1], axis=1)
    )
    proj = gather_dp(strip)
    teacher = lax.all_gather(teacher_in, TN, axis=0, tiled=False)

    lines = lax.dynamic_slice_in_dim(rotation, dpos * part, part, 0)
    index_row = lax.broadcasted_iota(jnp.int32, (own, own), 0)
    index_col = lax.broadcasted_iota(jnp.int32, (own, own), 1)
    table = parity_sign(index_row & index_col).astype(BF)
    mixed = jnp.dot(lines * (2 * signs - 1).astype(BF), table, preferred_element_type=F32)
    for axis in TN[::-1]:
        count = lax.axis_size(axis)
        for place in range(count.bit_length() - 1):
            other = lax.ppermute(mixed, axis, [(i, i ^ 1 << place) for i in range(count)])
            upper = lax.axis_index(axis) >> place & 1
            mixed = jnp.where(upper == 1, other - mixed, mixed + other)
    turned = gather_dp(mixed.astype(BF))

    normed = layer_norm(student_in.astype(F32)).astype(BF)
    predicted = jnp.dot(normed, head_weight, preferred_element_type=F32)
    image_nums = jnp.arange(image_count, dtype=jnp.int32)
    counts = jnp.sum((image_ids[None, :] == image_nums[:, None]).astype(F32), axis=1)
    own_ids = lax.dynamic_slice_in_dim(image_ids, dpos * rows, rows, 0)
    token_counts = jnp.sum(
        jnp.where(own_ids[:, None] == image_nums[None, :], counts[None, :], 0.0), axis=1, keepdims=True
    )
    token_weight = 1.0 / token_counts

    raw, stat = pl.pallas_call(
        project_kernel,
        out_shape=(jax.ShapeDtypeStruct((rows, own), BF), jax.ShapeDtypeStruct((rows, 2), F32)),
        compiler_params=pltpu.CompilerParams(vmem_limit_bytes=40 << 20),
        cost_estimate=pl.CostEstimate(flops=2 * rows * width * own, bytes_accessed=8 << 20, transcendentals=0),
    )(teacher, proj)
    pieces = jnp.stack(split3(stat.T)).reshape(6 * rows // own, own).astype(BF)
    spare = -pieces.shape[0] % 16
    packed = jnp.concatenate([raw, pieces, jnp.zeros((spare, own), BF)])
    gathered = lax.all_gather(packed, TN, axis=0, tiled=False)
    stats = gathered[:, rows : rows + pieces.shape[0], :].astype(F32).reshape(blocks, 3, 2, rows).sum(1)
    block_mean, block_spread = stats[:, 0], stats[:, 1]
    mean = jnp.mean(block_mean, axis=0)
    adjust = block_mean - mean
    variance = (jnp.sum(block_spread, axis=0) + own * jnp.sum(adjust * adjust, axis=0)) / width
    rstd = lax.rsqrt(variance + 1e-06)
    scale = 1.0 / (jnp.sqrt(F32(width)) * prev_scale)

    tall = own + 2 * depth + 16
    spaces = [pl.BlockSpec(memory_space=pltpu.SMEM)] * 2 + [pl.BlockSpec(memory_space=pltpu.VMEM)] * 9
    sent = pl.pallas_call(
        main_kernel,
        out_shape=jax.ShapeDtypeStruct((chunks, tall, part), BF),
        in_specs=spaces,
        out_specs=pl.BlockSpec(memory_space=pltpu.VMEM),
        scratch_shapes=[pltpu.VMEM((blocks, rows, own), BF)],
        compiler_params=pltpu.CompilerParams(vmem_limit_bytes=48 << 20),
        cost_estimate=pl.CostEstimate(flops=5 * rows * width * own, bytes_accessed=12 << 20, transcendentals=0),
    )(
        tpos.reshape(1),
        scale,
        gathered,
        adjust.T,
        rstd[:, None],
        final_gain.reshape(blocks, 1, own),
        mean_prev.reshape(blocks, 1, own),
        turned,
        predicted,
        token_weight,
        normed,
    )
    taken = lax.all_to_all(sent, DP, 0, 0, tiled=True)

    grad_own = jnp.sum(taken[:, own : own + 2 * depth, :].astype(F32), axis=0).astype(BF)
    grads = gather_direct(gather_direct(grad_own, "yh"), "z").reshape(chunks, 2, depth, part)
    grad_head = grads.transpose(0, 2, 1, 3).reshape(chunks * depth, own).astype(F32)

    tail = taken[:, own + 2 * depth :, :].astype(F32)
    sums_t = tail[:, 0:6].reshape(chunks, 2, 3, part).sum(2).reshape(chunks, own)
    loss = tail[:, 6:12].reshape(chunks, 2, 3, part).sum((0, 2)).reshape(own)
    sums_d = tail[:, 12:15].sum(1)
    new_mean = jnp.sum(sums_t, axis=0) / all_tokens
    mean_d = jnp.sum(sums_d, axis=0) / all_tokens
    off_t = sums_t / rows - new_mean
    off_d = sums_d / rows - mean_d
    between = lax.dot_general(
        off_t, off_d, (((0,), (0,)), ((), ())), precision=lax.Precision.HIGHEST, preferred_element_type=F32
    )
    within = jnp.sum(taken[:, :own, :].astype(F32), axis=0)
    new_cov = (within + between * rows) / all_tokens
    return (new_cov, new_mean, grad_head, loss / image_count)


def solution(mesh):
    z, y, x = 8, 4, 4
    if mesh.devices.size != 512:
        z, y, x = 2, mesh.shape["dp"] // 2, mesh.shape["tensor"] // 4
    inner = Mesh(mesh.devices.reshape(z, y, x, 2, 2), DP + TN)
    return jax.shard_map(
        body,
        mesh=inner,
        in_specs=(
            P(DP, TN),
            P(TN, DP),
            P(),
            P(),
            P(None, TN),
            P(TN),
            P(),
            P(DP, None),
            P(None, TN),
            P(),
        ),
        out_specs=(P(TN, DP), P(TN), P(None, TN), P(TN)),
        check_vma=False,
    )
```

```python
import jax
import jax.numpy as jnp
from jax import lax
from jax.experimental import pallas as pl
from jax.experimental.pallas import tpu as pltpu
from jax.sharding import Mesh
from jax.sharding import PartitionSpec as P

DP = ("z", "yh")
TN = ("x", "yl", "c")
IMAGE_SHARE = 128
BF = jnp.bfloat16
F32 = jnp.float32


def hold(value):
    return lax.reduce_precision(value, 8, 7)


def split3(value):
    high = hold(value)
    rest = value - high
    mid = hold(rest)
    return high, mid, rest - mid


def broadcast_gather(block, axes):
    count = lax.axis_size(axes)
    return lax.all_to_all(jnp.broadcast_to(block[None], (count,) + block.shape), axes, 0, 0, tiled=True)


def parity_sign(value):
    count = jnp.zeros_like(value)
    for place in range(16):
        count = count + (value >> place & 1)
    return 1 - 2 * (count % 2)


def layer_norm(values):
    centred = values - jnp.mean(values, axis=-1, keepdims=True)
    spread = jnp.mean(centred * centred, axis=-1, keepdims=True)
    return centred * lax.rsqrt(spread + 1e-06)


def project_kernel(x_ref, w_ref, out_ref, stat_ref):
    own = w_ref.shape[1]
    total = jnp.zeros(out_ref.shape, F32)
    for b in range(x_ref.shape[0]):
        total += jnp.dot(x_ref[b], w_ref[b * own : (b + 1) * own, :], preferred_element_type=F32)
    mean = jnp.sum(total, axis=1, keepdims=True) * (1.0 / own)
    centred = total - mean
    out_ref[...] = centred.astype(BF)
    spread = jnp.sum(centred * centred, axis=1, keepdims=True)
    lane = lax.broadcasted_iota(jnp.int32, stat_ref.shape, 1)
    stat_ref[...] = jnp.where(lane == 0, mean, spread)


def moment_kernel(
    pos_ref, mine_ref, other_ref, adj_ref, rstd_ref, gain_ref, prev_ref, rot_ref, sign_ref,
    out_ref, basis_ref, sums_ref, f_ref,
):
    blocks, rows, own = f_ref.shape
    part = out_ref.shape[2]
    core = lax.rem(pos_ref[0], 2)
    rstd = rstd_ref[...]
    total = jnp.zeros((rows, own), F32)
    for j in range(blocks):
        source, q, side = (mine_ref, j, core) if j < blocks // 2 else (other_ref, j - blocks // 2, 1 - core)
        b = 2 * q + side
        value = (source[q, :rows, :].astype(F32) + adj_ref[:, j : j + 1]) * rstd * gain_ref[b]
        feature = value.astype(BF)
        f_ref[b] = feature
        feature = feature.astype(F32)
        sums_ref[b] = jnp.sum(feature, axis=0, keepdims=True)
        shifted = (feature - prev_ref[b]).astype(BF)
        turn = rot_ref[pl.ds(pl.multiple_of(b * own, own), own), :]
        total += jnp.dot(shifted, turn, preferred_element_type=F32)
    basis_ref[...] = total.astype(BF) * sign_ref[...]
    own_t = f_ref[pos_ref[0]].astype(F32).T
    own_col = jnp.sum(own_t, axis=1, keepdims=True)
    own_t = own_t.astype(BF)
    for b in range(blocks):
        block = jnp.dot(own_t, f_ref[b], preferred_element_type=F32) - own_col * (sums_ref[b] * (1.0 / rows))
        block = block.astype(BF)
        for h in range(2):
            out_ref[2 * b + h] = block[:, h * part : (h + 1) * part]


def hadamard_kernel(scale_ref, basis_ref, table_ref, out_ref):
    blocks, few, own = basis_ref.shape
    flat = basis_ref[...].reshape(blocks * few, own)
    mixed = jnp.dot(flat, table_ref[...], preferred_element_type=F32) * scale_ref[0]
    parts = [mixed[b * few : (b + 1) * few] for b in range(blocks)]
    step = 1
    while step < blocks:
        parts = [
            parts[b - step] - parts[b] if b & step else parts[b] + parts[b + step] for b in range(blocks)
        ]
        step *= 2
    for b in range(blocks):
        out_ref[b] = parts[b].astype(BF)


def grad_kernel(pos_ref, target_ref, pred_ref, w_ref, normed_ref, sums_ref, out_ref):
    chunks, _, part = out_ref.shape
    depth = normed_ref.shape[1] // chunks
    residual = pred_ref[...] - target_ref[...].astype(F32)
    weighted = residual * w_ref[...]
    loss = jnp.sum(weighted * residual, axis=0, keepdims=True)
    grad = lax.dot_general(
        normed_ref[...], weighted.astype(BF), (((0,), (0,)), ((), ())), preferred_element_type=F32
    ).astype(BF)
    row = lax.broadcasted_iota(jnp.int32, (16, part), 0)

    def parts(value):
        high = value.astype(BF).astype(F32)
        rest = value - high
        mid = rest.astype(BF).astype(F32)
        return [high, mid, rest - mid]

    own_row = sums_ref[pos_ref[0]]
    fixed = []
    for h in range(2):
        fixed += parts(own_row[:, h * part : (h + 1) * part])
    for h in range(2):
        fixed += parts(loss[:, h * part : (h + 1) * part])
    for d in range(chunks):
        for h in range(2):
            out_ref[d, h * depth : (h + 1) * depth, :] = grad[
                d * depth : (d + 1) * depth, h * part : (h + 1) * part
            ]
        tile = jnp.zeros((16, part), F32)
        here = sums_ref[d // 2][:, (d % 2) * part : (d % 2 + 1) * part]
        for i, piece in enumerate(fixed + parts(here)):
            tile = jnp.where(row == i, piece, tile)
        out_ref[d, 2 * depth :, :] = tile.astype(BF)


def body(
    teacher_in,
    out_proj,
    final_gain,
    mean_prev,
    rotation,
    signs,
    prev_scale,
    student_in,
    head_weight,
    image_ids,
):
    rows, own = teacher_in.shape
    part = out_proj.shape[1]
    width = final_gain.shape[0]
    blocks = width // own
    chunks = width // part
    depth = student_in.shape[1] // chunks
    all_tokens = image_ids.shape[0]
    image_count = all_tokens // IMAGE_SHARE
    dpos = lax.axis_index(DP)
    tpos = lax.axis_index(TN)

    side = dpos % 2
    halves = out_proj.reshape(2, part, part)
    got = []
    for k in range(2):
        send = lax.dynamic_index_in_dim(halves, (side + k) % 2, 0, keepdims=False)
        route = []
        for d in range(chunks):
            for t in range(blocks):
                route.append((d * blocks + t, (2 * t + (d % 2 ^ k)) * blocks + d // 2))
        got.append(lax.ppermute(send, DP + TN, route))
    strip = jnp.where(
        side == 0, jnp.concatenate(got, axis=1), jnp.concatenate(got[::-1], axis=1)
    )
    proj = broadcast_gather(strip, DP).reshape(width, own)
    teacher = lax.all_gather(teacher_in, TN, axis=0, tiled=False)

    normed = layer_norm(student_in.astype(F32)).astype(BF)
    predicted = jnp.dot(normed, head_weight, preferred_element_type=F32)
    image_nums = jnp.arange(image_count, dtype=jnp.int32)
    counts = jnp.sum((image_ids[None, :] == image_nums[:, None]).astype(F32), axis=1)
    own_ids = lax.dynamic_slice_in_dim(image_ids, dpos * rows, rows, 0)
    token_counts = jnp.sum(
        jnp.where(own_ids[:, None] == image_nums[None, :], counts[None, :], 0.0), axis=1, keepdims=True
    )
    token_weight = 1.0 / token_counts

    raw, stat = pl.pallas_call(
        project_kernel,
        out_shape=(jax.ShapeDtypeStruct((rows, own), BF), jax.ShapeDtypeStruct((rows, 2), F32)),
        compiler_params=pltpu.CompilerParams(vmem_limit_bytes=40 << 20),
        cost_estimate=pl.CostEstimate(flops=2 * rows * width * own, bytes_accessed=8 << 20, transcendentals=0),
    )(teacher, proj)
    pieces = jnp.stack(split3(stat.T)).reshape(6 * rows // own, own).astype(BF)
    spare = -pieces.shape[0] % 16
    packed = jnp.concatenate([raw, pieces, jnp.zeros((spare, own), BF)])
    mine = broadcast_gather(packed, TN[:2])
    other = lax.ppermute(mine, "c", [(0, 1), (1, 0)])
    first = tpos % 2 == 0

    def unpack(block):
        tail = block[:, rows : rows + pieces.shape[0], :].astype(F32)
        return tail.reshape(blocks // 2, 3, 2, rows).sum(1)

    stat_mine, stat_other = unpack(mine), unpack(other)
    stats = jnp.stack(
        [jnp.where(first, stat_mine, stat_other), jnp.where(first, stat_other, stat_mine)], axis=1
    ).reshape(blocks, 2, rows)
    mean = jnp.mean(stats[:, 0], axis=0)
    adjust = stats[:, 0] - mean
    variance = (jnp.sum(stats[:, 1], axis=0) + own * jnp.sum(adjust * adjust, axis=0)) / width
    rstd = lax.rsqrt(variance + 1e-06)
    adjust = jnp.concatenate([stat_mine[:, 0], stat_other[:, 0]]) - mean
    scale = 1.0 / (jnp.sqrt(F32(width)) * prev_scale)
    index_row = lax.broadcasted_iota(jnp.int32, (own, own), 0)
    index_col = lax.broadcasted_iota(jnp.int32, (own, own), 1)
    table = parity_sign(index_row & index_col).astype(BF)

    smem, vmem = pl.BlockSpec(memory_space=pltpu.SMEM), pl.BlockSpec(memory_space=pltpu.VMEM)
    moment, basis, sums = pl.pallas_call(
        moment_kernel,
        out_shape=(
            jax.ShapeDtypeStruct((chunks, own, part), BF),
            jax.ShapeDtypeStruct((rows, own), BF),
            jax.ShapeDtypeStruct((blocks, 1, own), F32),
        ),
        in_specs=[smem] + [vmem] * 8,
        out_specs=(vmem,) * 3,
        scratch_shapes=[pltpu.VMEM((blocks, rows, own), BF)],
        compiler_params=pltpu.CompilerParams(vmem_limit_bytes=40 << 20),
        cost_estimate=pl.CostEstimate(flops=4 * rows * width * own, bytes_accessed=12 << 20, transcendentals=0),
    )(
        tpos.reshape(1),
        mine,
        other,
        adjust.T,
        rstd[:, None],
        final_gain.reshape(blocks, 1, own),
        mean_prev.reshape(blocks, 1, own),
        rotation,
        (2 * signs - 1).astype(BF)[None, :],
    )
    within = lax.psum_scatter(moment, "z", scatter_dimension=0, tiled=True)
    within = lax.psum_scatter(within, "yh", scatter_dimension=0, tiled=True)

    lines = lax.all_to_all(basis.reshape(blocks, rows // blocks, own), TN, 0, 0, tiled=True)
    lines = pl.pallas_call(
        hadamard_kernel,
        out_shape=jax.ShapeDtypeStruct(lines.shape, BF),
        in_specs=[smem, vmem, vmem],
        out_specs=vmem,
        compiler_params=pltpu.CompilerParams(vmem_limit_bytes=24 << 20),
    )(scale, lines, table)
    target = lax.all_to_all(lines, TN, 0, 0, tiled=True).reshape(rows, own)

    sent = pl.pallas_call(
        grad_kernel,
        out_shape=jax.ShapeDtypeStruct((chunks, 2 * depth + 16, part), BF),
        in_specs=[smem] + [vmem] * 5,
        out_specs=vmem,
        compiler_params=pltpu.CompilerParams(vmem_limit_bytes=24 << 20),
    )(tpos.reshape(1), target, predicted, token_weight, normed, sums)
    taken = lax.all_to_all(sent, DP, 0, 0, tiled=True)

    grad_own = jnp.sum(taken[:, : 2 * depth, :].astype(F32), axis=0).astype(BF)
    grads = broadcast_gather(grad_own, DP).reshape(chunks, 2, depth, part)
    grad_head = grads.transpose(0, 2, 1, 3).reshape(chunks * depth, own).astype(F32)

    tail = taken[:, 2 * depth :, :].astype(F32)
    sums_t = tail[:, 0:6].reshape(chunks, 2, 3, part).sum(2).reshape(chunks, own)
    loss = tail[:, 6:12].reshape(chunks, 2, 3, part).sum((0, 2)).reshape(own)
    sums_d = tail[:, 12:15].sum(1)
    new_mean = jnp.sum(sums_t, axis=0) / all_tokens
    mean_d = jnp.sum(sums_d, axis=0) / all_tokens
    off_t = sums_t / rows - new_mean
    off_d = sums_d / rows - mean_d
    between = lax.dot_general(
        off_t, off_d, (((0,), (0,)), ((), ())), precision=lax.Precision.HIGHEST, preferred_element_type=F32
    )
    new_cov = (within.reshape(own, part).astype(F32) + between * rows) / all_tokens
    return (new_cov, new_mean, grad_head, loss / image_count)


def solution(mesh):
    z, y, x = 8, 4, 4
    if mesh.devices.size != 512:
        z, y, x = 2, mesh.shape["dp"] // 2, mesh.shape["tensor"] // 4
    inner = Mesh(mesh.devices.reshape(z, y, x, 2, 2), DP + TN)
    return jax.shard_map(
        body,
        mesh=inner,
        in_specs=(
            P(DP, TN),
            P(TN, DP),
            P(),
            P(),
            P(None, TN),
            P(TN),
            P(),
            P(DP, None),
            P(None, TN),
            P(),
        ),
        out_specs=(P(TN, DP), P(TN), P(None, TN), P(TN)),
        check_vma=False,
    )
```

```python
import jax
import jax.numpy as jnp
from jax import lax
from jax.experimental import pallas as pl
from jax.experimental.pallas import tpu as pltpu
from jax.sharding import Mesh
from jax.sharding import PartitionSpec as P

DP = ("z", "yh")
TN = ("x", "yl", "c")
IMAGE_SHARE = 128
BF = jnp.bfloat16
F32 = jnp.float32


def hold(value):
    return lax.reduce_precision(value, 8, 7)


def split3(value):
    high = hold(value)
    rest = value - high
    mid = hold(rest)
    return high, mid, rest - mid


def broadcast_gather(block, axes):
    count = lax.axis_size(axes)
    return lax.all_to_all(jnp.broadcast_to(block[None], (count,) + block.shape), axes, 0, 0, tiled=True)


def shift(block, axis, step):
    count = lax.axis_size(axis)
    return lax.ppermute(block, axis, [(i, (i + step) % count) for i in range(count)])


def ring_gather(block, axis):
    count = lax.axis_size(axis)
    ahead, behind = [block], [block]
    for _ in range(count // 2 - 1):
        ahead.append(shift(ahead[-1], axis, -1))
        behind.append(shift(behind[-1], axis, 1))
    half = block.shape[0] // 2
    far = jnp.concatenate([shift(ahead[-1][:half], axis, -1), shift(behind[-1][half:], axis, 1)])
    blocks = ahead + [far] + behind[:0:-1]
    return lax.dynamic_slice_in_dim(jnp.stack(blocks + blocks), count - lax.axis_index(axis), count, 0)


def parity_sign(value):
    count = jnp.zeros_like(value)
    for place in range(16):
        count = count + (value >> place & 1)
    return 1 - 2 * (count % 2)


def layer_norm(values):
    centred = values - jnp.mean(values, axis=-1, keepdims=True)
    spread = jnp.mean(centred * centred, axis=-1, keepdims=True)
    return centred * lax.rsqrt(spread + 1e-06)


def project_kernel(x_ref, w_ref, out_ref, stat_ref):
    own = w_ref.shape[1]
    total = jnp.zeros(out_ref.shape, F32)
    for b in range(x_ref.shape[0]):
        total += jnp.dot(x_ref[b], w_ref[b * own : (b + 1) * own, :], preferred_element_type=F32)
    mean = jnp.sum(total, axis=1, keepdims=True) * (1.0 / own)
    centred = total - mean
    out_ref[...] = centred.astype(BF)
    spread = jnp.sum(centred * centred, axis=1, keepdims=True)
    lane = lax.broadcasted_iota(jnp.int32, stat_ref.shape, 1)
    stat_ref[...] = jnp.where(lane == 0, mean, spread)


def moment_kernel(
    pos_ref, mine_ref, other_ref, adj_ref, rstd_ref, gain_ref, prev_ref, rot_ref, sign_ref,
    out_ref, basis_ref, sums_ref, f_ref,
):
    blocks, rows, own = f_ref.shape
    part = out_ref.shape[2]
    core = lax.rem(pos_ref[0], 2)
    rstd = rstd_ref[...]
    total = jnp.zeros((rows, own), F32)
    for j in range(blocks):
        source, q, side = (mine_ref, j, core) if j < blocks // 2 else (other_ref, j - blocks // 2, 1 - core)
        b = 2 * q + side
        value = (source[q, :rows, :].astype(F32) + adj_ref[:, j : j + 1]) * rstd * gain_ref[b]
        feature = value.astype(BF)
        f_ref[b] = feature
        feature = feature.astype(F32)
        sums_ref[b] = jnp.sum(feature, axis=0, keepdims=True)
        shifted = (feature - prev_ref[b]).astype(BF)
        turn = rot_ref[pl.ds(pl.multiple_of(b * own, own), own), :]
        total += jnp.dot(shifted, turn, preferred_element_type=F32)
    basis_ref[...] = total.astype(BF) * sign_ref[...]
    own_t = f_ref[pos_ref[0]].astype(F32).T
    own_col = jnp.sum(own_t, axis=1, keepdims=True)
    own_t = own_t.astype(BF)
    for b in range(blocks):
        block = jnp.dot(own_t, f_ref[b], preferred_element_type=F32) - own_col * (sums_ref[b] * (1.0 / rows))
        block = block.astype(BF)
        for h in range(2):
            out_ref[2 * b + h] = block[:, h * part : (h + 1) * part]


def hadamard_kernel(scale_ref, basis_ref, table_ref, out_ref):
    blocks, few, own = basis_ref.shape
    flat = basis_ref[...].reshape(blocks * few, own)
    mixed = jnp.dot(flat, table_ref[...], preferred_element_type=F32) * scale_ref[0]
    parts = [mixed[b * few : (b + 1) * few] for b in range(blocks)]
    step = 1
    while step < blocks:
        parts = [
            parts[b - step] - parts[b] if b & step else parts[b] + parts[b + step] for b in range(blocks)
        ]
        step *= 2
    for b in range(blocks):
        out_ref[b] = parts[b].astype(BF)


def grad_kernel(pos_ref, target_ref, pred_ref, w_ref, normed_ref, sums_ref, out_ref):
    chunks, _, part = out_ref.shape
    depth = normed_ref.shape[1] // chunks
    residual = pred_ref[...] - target_ref[...].astype(F32)
    weighted = residual * w_ref[...]
    loss = jnp.sum(weighted * residual, axis=0, keepdims=True)
    grad = lax.dot_general(
        normed_ref[...], weighted.astype(BF), (((0,), (0,)), ((), ())), preferred_element_type=F32
    ).astype(BF)
    row = lax.broadcasted_iota(jnp.int32, (16, part), 0)

    def parts(value):
        high = value.astype(BF).astype(F32)
        rest = value - high
        mid = rest.astype(BF).astype(F32)
        return [high, mid, rest - mid]

    own_row = sums_ref[pos_ref[0]]
    fixed = []
    for h in range(2):
        fixed += parts(own_row[:, h * part : (h + 1) * part])
    for h in range(2):
        fixed += parts(loss[:, h * part : (h + 1) * part])
    for d in range(chunks):
        for h in range(2):
            out_ref[d, h * depth : (h + 1) * depth, :] = grad[
                d * depth : (d + 1) * depth, h * part : (h + 1) * part
            ]
        tile = jnp.zeros((16, part), F32)
        here = sums_ref[d // 2][:, (d % 2) * part : (d % 2 + 1) * part]
        for i, piece in enumerate(fixed + parts(here)):
            tile = jnp.where(row == i, piece, tile)
        out_ref[d, 2 * depth :, :] = tile.astype(BF)


def place_kernel(in_ref, out_ref):
    chunks, tall, part = in_ref.shape
    depth = tall // 2
    for d in range(chunks):
        for h in range(2):
            out_ref[d * depth : (d + 1) * depth, h * part : (h + 1) * part] = in_ref[
                d, h * depth : (h + 1) * depth, :
            ].astype(F32)


def body(
    teacher_in,
    out_proj,
    final_gain,
    mean_prev,
    rotation,
    signs,
    prev_scale,
    student_in,
    head_weight,
    image_ids,
):
    rows, own = teacher_in.shape
    part = out_proj.shape[1]
    width = final_gain.shape[0]
    blocks = width // own
    chunks = width // part
    depth = student_in.shape[1] // chunks
    all_tokens = image_ids.shape[0]
    image_count = all_tokens // IMAGE_SHARE
    dpos = lax.axis_index(DP)
    tpos = lax.axis_index(TN)

    side = dpos % 2
    halves = out_proj.reshape(2, part, part)
    got = []
    for k in range(2):
        send = lax.dynamic_index_in_dim(halves, (side + k) % 2, 0, keepdims=False)
        route = []
        for d in range(chunks):
            for t in range(blocks):
                route.append((d * blocks + t, (2 * t + (d % 2 ^ k)) * blocks + d // 2))
        got.append(lax.ppermute(send, DP + TN, route))
    strip = jnp.where(
        side == 0, jnp.concatenate(got, axis=1), jnp.concatenate(got[::-1], axis=1)
    )
    near = broadcast_gather(strip, "yh")
    proj = ring_gather(near.reshape(-1, own), "z").reshape(width, own)
    teacher = lax.all_gather(teacher_in, TN, axis=0, tiled=False)

    normed = layer_norm(student_in.astype(F32)).astype(BF)
    predicted = jnp.dot(normed, head_weight, preferred_element_type=F32)
    image_nums = jnp.arange(image_count, dtype=jnp.int32)
    counts = jnp.sum((image_ids[None, :] == image_nums[:, None]).astype(F32), axis=1)
    own_ids = lax.dynamic_slice_in_dim(image_ids, dpos * rows, rows, 0)
    token_counts = jnp.sum(
        jnp.where(own_ids[:, None] == image_nums[None, :], counts[None, :], 0.0), axis=1, keepdims=True
    )
    token_weight = 1.0 / token_counts

    raw, stat = pl.pallas_call(
        project_kernel,
        out_shape=(jax.ShapeDtypeStruct((rows, own), BF), jax.ShapeDtypeStruct((rows, 2), F32)),
        compiler_params=pltpu.CompilerParams(vmem_limit_bytes=40 << 20),
        cost_estimate=pl.CostEstimate(flops=2 * rows * width * own, bytes_accessed=8 << 20, transcendentals=0),
    )(teacher, proj)
    pieces = jnp.stack(split3(stat.T)).reshape(6 * rows // own, own).astype(BF)
    spare = -pieces.shape[0] % 16
    packed = jnp.concatenate([raw, pieces, jnp.zeros((spare, own), BF)])
    mine = broadcast_gather(packed, TN[:2])
    other = lax.ppermute(mine, "c", [(0, 1), (1, 0)])
    first = tpos % 2 == 0

    def unpack(block):
        tail = block[:, rows : rows + pieces.shape[0], :].astype(F32)
        return tail.reshape(blocks // 2, 3, 2, rows).sum(1)

    stat_mine, stat_other = unpack(mine), unpack(other)
    stats = jnp.stack(
        [jnp.where(first, stat_mine, stat_other), jnp.where(first, stat_other, stat_mine)], axis=1
    ).reshape(blocks, 2, rows)
    mean = jnp.mean(stats[:, 0], axis=0)
    adjust = stats[:, 0] - mean
    variance = (jnp.sum(stats[:, 1], axis=0) + own * jnp.sum(adjust * adjust, axis=0)) / width
    rstd = lax.rsqrt(variance + 1e-06)
    adjust = jnp.concatenate([stat_mine[:, 0], stat_other[:, 0]]) - mean
    scale = 1.0 / (jnp.sqrt(F32(width)) * prev_scale)
    index_row = lax.broadcasted_iota(jnp.int32, (own, own), 0)
    index_col = lax.broadcasted_iota(jnp.int32, (own, own), 1)
    table = parity_sign(index_row & index_col).astype(BF)

    smem, vmem = pl.BlockSpec(memory_space=pltpu.SMEM), pl.BlockSpec(memory_space=pltpu.VMEM)
    moment, basis, sums = pl.pallas_call(
        moment_kernel,
        out_shape=(
            jax.ShapeDtypeStruct((chunks, own, part), BF),
            jax.ShapeDtypeStruct((rows, own), BF),
            jax.ShapeDtypeStruct((blocks, 1, own), F32),
        ),
        in_specs=[smem] + [vmem] * 8,
        out_specs=(vmem,) * 3,
        scratch_shapes=[pltpu.VMEM((blocks, rows, own), BF)],
        compiler_params=pltpu.CompilerParams(vmem_limit_bytes=40 << 20),
        cost_estimate=pl.CostEstimate(flops=4 * rows * width * own, bytes_accessed=12 << 20, transcendentals=0),
    )(
        tpos.reshape(1),
        mine,
        other,
        adjust.T,
        rstd[:, None],
        final_gain.reshape(blocks, 1, own),
        mean_prev.reshape(blocks, 1, own),
        rotation,
        (2 * signs - 1).astype(BF)[None, :],
    )
    within = lax.psum_scatter(moment, "z", scatter_dimension=0, tiled=True)

    lines = lax.all_to_all(basis.reshape(blocks, rows // blocks, own), TN, 0, 0, tiled=True)
    lines = pl.pallas_call(
        hadamard_kernel,
        out_shape=jax.ShapeDtypeStruct(lines.shape, BF),
        in_specs=[smem, vmem, vmem],
        out_specs=vmem,
        compiler_params=pltpu.CompilerParams(vmem_limit_bytes=24 << 20),
    )(scale, lines, table)
    target = lax.all_to_all(lines, TN, 0, 0, tiled=True).reshape(rows, own)

    sent = pl.pallas_call(
        grad_kernel,
        out_shape=jax.ShapeDtypeStruct((chunks, 2 * depth + 16, part), BF),
        in_specs=[smem] + [vmem] * 5,
        out_specs=vmem,
        compiler_params=pltpu.CompilerParams(vmem_limit_bytes=24 << 20),
    )(tpos.reshape(1), target, predicted, token_weight, normed, sums)
    taken = lax.all_to_all(sent, DP, 0, 0, tiled=True)

    grad_own = jnp.sum(taken[:, : 2 * depth, :].astype(F32), axis=0).astype(BF)
    within, grad_own = lax.optimization_barrier((within, grad_own))
    within = lax.psum_scatter(within, "yh", scatter_dimension=0, tiled=True)
    grad_head = pl.pallas_call(
        place_kernel,
        out_shape=jax.ShapeDtypeStruct((chunks * depth, own), F32),
        in_specs=[vmem],
        out_specs=vmem,
    )(broadcast_gather(grad_own, DP))

    tail = taken[:, 2 * depth :, :].astype(F32)
    sums_t = tail[:, 0:6].reshape(chunks, 2, 3, part).sum(2).reshape(chunks, own)
    loss = tail[:, 6:12].reshape(chunks, 2, 3, part).sum((0, 2)).reshape(own)
    sums_d = tail[:, 12:15].sum(1)
    new_mean = jnp.sum(sums_t, axis=0) / all_tokens
    mean_d = jnp.sum(sums_d, axis=0) / all_tokens
    off_t = sums_t / rows - new_mean
    off_d = sums_d / rows - mean_d
    between = lax.dot_general(
        off_t, off_d, (((0,), (0,)), ((), ())), precision=lax.Precision.HIGHEST, preferred_element_type=F32
    )
    new_cov = (within.reshape(own, part).astype(F32) + between * rows) / all_tokens
    return (new_cov, new_mean, grad_head, loss / image_count)


def solution(mesh):
    z, y, x = 8, 4, 4
    if mesh.devices.size != 512:
        z, y, x = 2, mesh.shape["dp"] // 2, mesh.shape["tensor"] // 4
    inner = Mesh(mesh.devices.reshape(z, y, x, 2, 2), DP + TN)
    return jax.shard_map(
        body,
        mesh=inner,
        in_specs=(
            P(DP, TN),
            P(TN, DP),
            P(),
            P(),
            P(None, TN),
            P(TN),
            P(),
            P(DP, None),
            P(None, TN),
            P(),
        ),
        out_specs=(P(TN, DP), P(TN), P(None, TN), P(TN)),
        check_vma=False,
    )
```

```python
import jax
import jax.numpy as jnp
from jax import lax
from jax.experimental import pallas as pl
from jax.experimental.pallas import tpu as pltpu
from jax.sharding import Mesh
from jax.sharding import PartitionSpec as P

DP = ("z", "yh")
TN = ("x", "yl", "c")
IMAGE_SHARE = 128
BF = jnp.bfloat16
F32 = jnp.float32


def hold(value):
    return lax.reduce_precision(value, 8, 7)


def split3(value):
    high = hold(value)
    rest = value - high
    mid = hold(rest)
    return high, mid, rest - mid


def broadcast_gather(block, axes):
    count = lax.axis_size(axes)
    return lax.all_to_all(jnp.broadcast_to(block[None], (count,) + block.shape), axes, 0, 0, tiled=True)


def shift(block, axis, step):
    count = lax.axis_size(axis)
    return lax.ppermute(block, axis, [(i, (i + step) % count) for i in range(count)])


def tensor_gather(block):
    mine = broadcast_gather(block, TN[:2])
    return mine, lax.ppermute(mine, "c", [(0, 1), (1, 0)])


def parity_sign(value):
    count = jnp.zeros_like(value)
    for place in range(16):
        count = count + (value >> place & 1)
    return 1 - 2 * (count % 2)


def layer_norm(values):
    centred = values - jnp.mean(values, axis=-1, keepdims=True)
    spread = jnp.mean(centred * centred, axis=-1, keepdims=True)
    return centred * lax.rsqrt(spread + 1e-06)


def project_kernel(pos_ref, mine_ref, other_ref, w_ref, out_ref, stat_ref):
    own = w_ref.shape[1]
    core = lax.rem(pos_ref[0], 2)
    total = jnp.zeros(out_ref.shape, F32)
    for source, side in ((mine_ref, core), (other_ref, 1 - core)):
        for q in range(source.shape[0]):
            start = pl.multiple_of((2 * q + side) * own, own)
            total += jnp.dot(source[q], w_ref[pl.ds(start, own), :], preferred_element_type=F32)
    mean = jnp.sum(total, axis=1, keepdims=True) * (1.0 / own)
    centred = total - mean
    out_ref[...] = centred.astype(BF)
    spread = jnp.sum(centred * centred, axis=1, keepdims=True)
    lane = lax.broadcasted_iota(jnp.int32, stat_ref.shape, 1)
    stat_ref[...] = jnp.where(lane == 0, mean, spread)


def feature_kernel(
    pos_ref, mine_ref, other_ref, adj_ref, rstd_ref, gain_ref, prev_ref, rot_ref, sign_ref,
    f_ref, basis_ref, sums_ref,
):
    blocks, rows, own = f_ref.shape
    core = lax.rem(pos_ref[0], 2)
    rstd = rstd_ref[...]
    total = jnp.zeros((rows, own), F32)
    for j in range(blocks):
        source, q, side = (mine_ref, j, core) if j < blocks // 2 else (other_ref, j - blocks // 2, 1 - core)
        b = 2 * q + side
        value = (source[q, :rows, :].astype(F32) + adj_ref[:, j : j + 1]) * rstd * gain_ref[b]
        feature = value.astype(BF)
        f_ref[b] = feature
        feature = feature.astype(F32)
        sums_ref[b] = jnp.sum(feature, axis=0, keepdims=True)
        shifted = (feature - prev_ref[b]).astype(BF)
        turn = rot_ref[pl.ds(pl.multiple_of(b * own, own), own), :]
        total += jnp.dot(shifted, turn, preferred_element_type=F32)
    basis_ref[...] = total.astype(BF) * sign_ref[...]


def moment_kernel(pos_ref, f_ref, sums_ref, out_ref):
    blocks, rows, own = f_ref.shape
    part = out_ref.shape[2]
    own_t = f_ref[pos_ref[0]].astype(F32).T
    own_col = jnp.sum(own_t, axis=1, keepdims=True)
    own_t = own_t.astype(BF)
    for b in range(blocks):
        block = jnp.dot(own_t, f_ref[b], preferred_element_type=F32) - own_col * (sums_ref[b] * (1.0 / rows))
        block = block.astype(BF)
        for h in range(2):
            out_ref[2 * b + h] = block[:, h * part : (h + 1) * part]


def hadamard_kernel(scale_ref, basis_ref, table_ref, out_ref):
    blocks, few, own = basis_ref.shape
    flat = basis_ref[...].reshape(blocks * few, own)
    mixed = jnp.dot(flat, table_ref[...], preferred_element_type=F32) * scale_ref[0]
    parts = [mixed[b * few : (b + 1) * few] for b in range(blocks)]
    step = 1
    while step < blocks:
        parts = [
            parts[b - step] - parts[b] if b & step else parts[b] + parts[b + step] for b in range(blocks)
        ]
        step *= 2
    for b in range(blocks):
        out_ref[b] = parts[b].astype(BF)


def grad_kernel(pos_ref, target_ref, pred_ref, w_ref, normed_ref, sums_ref, out_ref):
    chunks, _, part = out_ref.shape
    depth = normed_ref.shape[1] // chunks
    residual = pred_ref[...] - target_ref[...].astype(F32)
    weighted = residual * w_ref[...]
    loss = jnp.sum(weighted * residual, axis=0, keepdims=True)
    grad = lax.dot_general(
        normed_ref[...], weighted.astype(BF), (((0,), (0,)), ((), ())), preferred_element_type=F32
    ).astype(BF)
    row = lax.broadcasted_iota(jnp.int32, (16, part), 0)

    def parts(value):
        high = value.astype(BF).astype(F32)
        rest = value - high
        mid = rest.astype(BF).astype(F32)
        return [high, mid, rest - mid]

    own_row = sums_ref[pos_ref[0]]
    fixed = []
    for h in range(2):
        fixed += parts(own_row[:, h * part : (h + 1) * part])
    for h in range(2):
        fixed += parts(loss[:, h * part : (h + 1) * part])
    for d in range(chunks):
        for h in range(2):
            out_ref[d, h * depth : (h + 1) * depth, :] = grad[
                d * depth : (d + 1) * depth, h * part : (h + 1) * part
            ]
        tile = jnp.zeros((16, part), F32)
        here = sums_ref[d // 2][:, (d % 2) * part : (d % 2 + 1) * part]
        for i, piece in enumerate(fixed + parts(here)):
            tile = jnp.where(row == i, piece, tile)
        out_ref[d, 2 * depth :, :] = tile.astype(BF)


def place_kernel(in_ref, out_ref):
    chunks, tall, part = in_ref.shape
    depth = tall // 2
    for d in range(chunks):
        for h in range(2):
            out_ref[d * depth : (d + 1) * depth, h * part : (h + 1) * part] = in_ref[
                d, h * depth : (h + 1) * depth, :
            ].astype(F32)


def body(
    teacher_in,
    out_proj,
    final_gain,
    mean_prev,
    rotation,
    signs,
    prev_scale,
    student_in,
    head_weight,
    image_ids,
):
    rows, own = teacher_in.shape
    part = out_proj.shape[1]
    width = final_gain.shape[0]
    blocks = width // own
    chunks = width // part
    depth = student_in.shape[1] // chunks
    all_tokens = image_ids.shape[0]
    image_count = all_tokens // IMAGE_SHARE
    dpos = lax.axis_index(DP)
    tpos = lax.axis_index(TN)

    side = dpos % 2
    halves = out_proj.reshape(2, part, part)
    got = []
    for k in range(2):
        send = lax.dynamic_index_in_dim(halves, (side + k) % 2, 0, keepdims=False)
        route = []
        for d in range(chunks):
            for t in range(blocks):
                route.append((d * blocks + t, (2 * t + (d % 2 ^ k)) * blocks + d // 2))
        got.append(lax.ppermute(send, DP + TN, route))
    strip = jnp.where(
        side == 0, jnp.concatenate(got, axis=1), jnp.concatenate(got[::-1], axis=1)
    )
    near = broadcast_gather(strip, "yh")
    proj = lax.all_gather(near.reshape(-1, own), "z", axis=0, tiled=True)
    teacher, _ = lax.optimization_barrier((teacher_in, near))
    teacher = tensor_gather(teacher)

    normed = layer_norm(student_in.astype(F32)).astype(BF)
    predicted = jnp.dot(normed, head_weight, preferred_element_type=F32)
    image_nums = jnp.arange(image_count, dtype=jnp.int32)
    counts = jnp.sum((image_ids[None, :] == image_nums[:, None]).astype(F32), axis=1)
    own_ids = lax.dynamic_slice_in_dim(image_ids, dpos * rows, rows, 0)
    token_counts = jnp.sum(
        jnp.where(own_ids[:, None] == image_nums[None, :], counts[None, :], 0.0), axis=1, keepdims=True
    )
    token_weight = 1.0 / token_counts

    smem, vmem = pl.BlockSpec(memory_space=pltpu.SMEM), pl.BlockSpec(memory_space=pltpu.VMEM)
    position = tpos.reshape(1)
    raw, stat = pl.pallas_call(
        project_kernel,
        out_shape=(jax.ShapeDtypeStruct((rows, own), BF), jax.ShapeDtypeStruct((rows, 2), F32)),
        in_specs=[smem, vmem, vmem, vmem],
        out_specs=(vmem, vmem),
        compiler_params=pltpu.CompilerParams(vmem_limit_bytes=40 << 20),
        cost_estimate=pl.CostEstimate(flops=2 * rows * width * own, bytes_accessed=8 << 20, transcendentals=0),
    )(position, *teacher, proj)
    pieces = jnp.stack(split3(stat.T)).reshape(6 * rows // own, own).astype(BF)
    spare = -pieces.shape[0] % 16
    packed = jnp.concatenate([raw, pieces, jnp.zeros((spare, own), BF)])
    mine, other = tensor_gather(packed)
    first = tpos % 2 == 0

    def unpack(block):
        tail = block[:, rows : rows + pieces.shape[0], :].astype(F32)
        return tail.reshape(blocks // 2, 3, 2, rows).sum(1)

    stat_mine, stat_other = unpack(mine), unpack(other)
    stats = jnp.stack(
        [jnp.where(first, stat_mine, stat_other), jnp.where(first, stat_other, stat_mine)], axis=1
    ).reshape(blocks, 2, rows)
    mean = jnp.mean(stats[:, 0], axis=0)
    adjust = stats[:, 0] - mean
    variance = (jnp.sum(stats[:, 1], axis=0) + own * jnp.sum(adjust * adjust, axis=0)) / width
    rstd = lax.rsqrt(variance + 1e-06)
    adjust = jnp.concatenate([stat_mine[:, 0], stat_other[:, 0]]) - mean
    scale = 1.0 / (jnp.sqrt(F32(width)) * prev_scale)
    index_row = lax.broadcasted_iota(jnp.int32, (own, own), 0)
    index_col = lax.broadcasted_iota(jnp.int32, (own, own), 1)
    table = parity_sign(index_row & index_col).astype(BF)

    features, basis, sums = pl.pallas_call(
        feature_kernel,
        out_shape=(
            jax.ShapeDtypeStruct((blocks, rows, own), BF),
            jax.ShapeDtypeStruct((rows, own), BF),
            jax.ShapeDtypeStruct((blocks, 1, own), F32),
        ),
        in_specs=[smem] + [vmem] * 8,
        out_specs=(vmem,) * 3,
        compiler_params=pltpu.CompilerParams(vmem_limit_bytes=40 << 20),
        cost_estimate=pl.CostEstimate(flops=2 * rows * width * own, bytes_accessed=12 << 20, transcendentals=0),
    )(
        position,
        mine,
        other,
        adjust.T,
        rstd[:, None],
        final_gain.reshape(blocks, 1, own),
        mean_prev.reshape(blocks, 1, own),
        rotation,
        (2 * signs - 1).astype(BF)[None, :],
    )
    lines = lax.all_to_all(basis.reshape(blocks, rows // blocks, own), TN, 0, 0, tiled=True)
    moment = pl.pallas_call(
        moment_kernel,
        out_shape=jax.ShapeDtypeStruct((chunks, own, part), BF),
        in_specs=[smem, vmem, vmem],
        out_specs=vmem,
        compiler_params=pltpu.CompilerParams(vmem_limit_bytes=24 << 20),
        cost_estimate=pl.CostEstimate(flops=2 * rows * width * own, bytes_accessed=6 << 20, transcendentals=0),
    )(position, features, sums)
    within = lax.psum_scatter(moment, "z", scatter_dimension=0, tiled=True)

    lines = pl.pallas_call(
        hadamard_kernel,
        out_shape=jax.ShapeDtypeStruct(lines.shape, BF),
        in_specs=[smem, vmem, vmem],
        out_specs=vmem,
        compiler_params=pltpu.CompilerParams(vmem_limit_bytes=24 << 20),
    )(scale, lines, table)
    target = lax.all_to_all(lines, TN, 0, 0, tiled=True).reshape(rows, own)

    sent = pl.pallas_call(
        grad_kernel,
        out_shape=jax.ShapeDtypeStruct((chunks, 2 * depth + 16, part), BF),
        in_specs=[smem] + [vmem] * 5,
        out_specs=vmem,
        compiler_params=pltpu.CompilerParams(vmem_limit_bytes=24 << 20),
    )(position, target, predicted, token_weight, normed, sums)
    taken = lax.all_to_all(sent, DP, 0, 0, tiled=True)

    grad_own = jnp.sum(taken[:, : 2 * depth, :].astype(F32), axis=0).astype(BF)
    within, grad_own = lax.optimization_barrier((within, grad_own))
    places, here = lax.axis_size("yh"), lax.axis_index("yh")
    within_sum = within[here].astype(F32)
    for k in range(1, places):
        within_sum += shift(within[(here + k) % places], "yh", k).astype(F32)
    grad_head = pl.pallas_call(
        place_kernel,
        out_shape=jax.ShapeDtypeStruct((chunks * depth, own), F32),
        in_specs=[vmem],
        out_specs=vmem,
    )(broadcast_gather(grad_own, DP))

    tail = taken[:, 2 * depth :, :].astype(F32)
    sums_t = tail[:, 0:6].reshape(chunks, 2, 3, part).sum(2).reshape(chunks, own)
    loss = tail[:, 6:12].reshape(chunks, 2, 3, part).sum((0, 2)).reshape(own)
    sums_d = tail[:, 12:15].sum(1)
    new_mean = jnp.sum(sums_t, axis=0) / all_tokens
    mean_d = jnp.sum(sums_d, axis=0) / all_tokens
    off_t = sums_t / rows - new_mean
    off_d = sums_d / rows - mean_d
    between = lax.dot_general(
        off_t, off_d, (((0,), (0,)), ((), ())), precision=lax.Precision.HIGHEST, preferred_element_type=F32
    )
    new_cov = (within_sum + between * rows) / all_tokens
    return (new_cov, new_mean, grad_head, loss / image_count)


def solution(mesh):
    z, y, x = 8, 4, 4
    if mesh.devices.size != 512:
        z, y, x = 2, mesh.shape["dp"] // 2, mesh.shape["tensor"] // 4
    inner = Mesh(mesh.devices.reshape(z, y, x, 2, 2), DP + TN)
    return jax.shard_map(
        body,
        mesh=inner,
        in_specs=(
            P(DP, TN),
            P(TN, DP),
            P(),
            P(),
            P(None, TN),
            P(TN),
            P(),
            P(DP, None),
            P(None, TN),
            P(),
        ),
        out_specs=(P(TN, DP), P(TN), P(None, TN), P(TN)),
        check_vma=False,
    )
```

```python
import jax
import jax.numpy as jnp
from jax import lax
from jax.experimental import pallas as pl
from jax.experimental.pallas import tpu as pltpu
from jax.sharding import Mesh
from jax.sharding import PartitionSpec as P

DP = ("z", "yh")
TN = ("x", "yl", "c")
IMAGE_SHARE = 128
BF = jnp.bfloat16
F32 = jnp.float32


def hold(value):
    return lax.reduce_precision(value, 8, 7)


def split3(value):
    high = hold(value)
    rest = value - high
    mid = hold(rest)
    return high, mid, rest - mid


def broadcast_gather(block, axes):
    count = lax.axis_size(axes)
    return lax.all_to_all(jnp.broadcast_to(block[None], (count,) + block.shape), axes, 0, 0, tiled=True)


def shift(block, axis, step):
    count = lax.axis_size(axis)
    return lax.ppermute(block, axis, [(i, (i + step) % count) for i in range(count)])


def tensor_gather(block):
    mine = broadcast_gather(block, TN[:2])
    half = mine.shape[0] // 2
    return mine, [lax.ppermute(part, "c", [(0, 1), (1, 0)]) for part in (mine[:half], mine[half:])]


def parity_sign(value):
    count = jnp.zeros_like(value)
    for place in range(16):
        count = count + (value >> place & 1)
    return 1 - 2 * (count % 2)


def layer_norm(values):
    centred = values - jnp.mean(values, axis=-1, keepdims=True)
    spread = jnp.mean(centred * centred, axis=-1, keepdims=True)
    return centred * lax.rsqrt(spread + 1e-06)


def project_kernel(x_ref, w_ref, out_ref, stat_ref):
    own = w_ref.shape[1]
    total = jnp.zeros(out_ref.shape, F32)
    for b in range(x_ref.shape[0]):
        total += jnp.dot(x_ref[b], w_ref[b * own : (b + 1) * own, :], preferred_element_type=F32)
    mean = jnp.sum(total, axis=1, keepdims=True) * (1.0 / own)
    centred = total - mean
    out_ref[...] = centred.astype(BF)
    spread = jnp.sum(centred * centred, axis=1, keepdims=True)
    lane = lax.broadcasted_iota(jnp.int32, stat_ref.shape, 1)
    stat_ref[...] = jnp.where(lane == 0, mean, spread)


def feature_kernel(pos_ref, mine_ref, low_ref, high_ref, adj_ref, rstd_ref, gain_ref, f_ref, sums_ref):
    blocks, rows, _ = f_ref.shape
    core = lax.rem(pos_ref[0], 2)
    rstd = rstd_ref[...]
    half = blocks // 4
    for j in range(blocks):
        q = j % (2 * half)
        b = 2 * q + (core if j < 2 * half else 1 - core)
        source = mine_ref if j < 2 * half else low_ref if q < half else high_ref
        place = q if j < 2 * half else q % half
        value = (source[place, :rows, :].astype(F32) + adj_ref[:, j : j + 1]) * rstd * gain_ref[b]
        feature = value.astype(BF)
        f_ref[b] = feature
        sums_ref[b] = jnp.sum(feature.astype(F32), axis=0, keepdims=True)


def moment_kernel(pos_ref, f_ref, sums_ref, out_ref):
    blocks, rows, own = f_ref.shape
    part = out_ref.shape[2]
    own_t = f_ref[pos_ref[0]].astype(F32).T
    own_col = jnp.sum(own_t, axis=1, keepdims=True)
    own_t = own_t.astype(BF)
    for b in range(blocks):
        block = jnp.dot(own_t, f_ref[b], preferred_element_type=F32) - own_col * (sums_ref[b] * (1.0 / rows))
        block = block.astype(BF)
        for h in range(2):
            out_ref[2 * b + h] = block[:, h * part : (h + 1) * part]


def hadamard_kernel(scale_ref, basis_ref, table_ref, out_ref):
    blocks, few, own = basis_ref.shape
    flat = basis_ref[...].reshape(blocks * few, own)
    mixed = jnp.dot(flat, table_ref[...], preferred_element_type=F32) * scale_ref[0]
    parts = [mixed[b * few : (b + 1) * few] for b in range(blocks)]
    step = 1
    while step < blocks:
        parts = [
            parts[b - step] - parts[b] if b & step else parts[b] + parts[b + step] for b in range(blocks)
        ]
        step *= 2
    for b in range(blocks):
        out_ref[b] = parts[b].astype(BF)


def grad_kernel(pos_ref, f_ref, prev_ref, turn_ref, pred_ref, w_ref, normed_ref, sums_ref, out_ref):
    chunks, _, part = out_ref.shape
    blocks, _, own = f_ref.shape
    depth = normed_ref.shape[1] // chunks
    target = jnp.zeros(pred_ref.shape, F32)
    for b in range(blocks):
        shifted = (f_ref[b].astype(F32) - prev_ref[b]).astype(BF)
        target += jnp.dot(shifted, turn_ref[b * own : (b + 1) * own, :], preferred_element_type=F32)
    residual = pred_ref[...] - target
    weighted = residual * w_ref[...]
    loss = jnp.sum(weighted * residual, axis=0, keepdims=True)
    grad = lax.dot_general(
        normed_ref[...], weighted.astype(BF), (((0,), (0,)), ((), ())), preferred_element_type=F32
    ).astype(BF)
    row = lax.broadcasted_iota(jnp.int32, (16, part), 0)

    def parts(value):
        high = value.astype(BF).astype(F32)
        rest = value - high
        mid = rest.astype(BF).astype(F32)
        return [high, mid, rest - mid]

    own_row = sums_ref[pos_ref[0]]
    fixed = []
    for h in range(2):
        fixed += parts(own_row[:, h * part : (h + 1) * part])
    for h in range(2):
        fixed += parts(loss[:, h * part : (h + 1) * part])
    for d in range(chunks):
        for h in range(2):
            out_ref[d, h * depth : (h + 1) * depth, :] = grad[
                d * depth : (d + 1) * depth, h * part : (h + 1) * part
            ]
        tile = jnp.zeros((16, part), F32)
        here = sums_ref[d // 2][:, (d % 2) * part : (d % 2 + 1) * part]
        for i, piece in enumerate(fixed + parts(here)):
            tile = jnp.where(row == i, piece, tile)
        out_ref[d, 2 * depth :, :] = tile.astype(BF)


def place_kernel(in_ref, out_ref):
    chunks, tall, part = in_ref.shape
    depth = tall // 2
    for d in range(chunks):
        for h in range(2):
            out_ref[d * depth : (d + 1) * depth, h * part : (h + 1) * part] = in_ref[
                d, h * depth : (h + 1) * depth, :
            ].astype(F32)


def body(
    teacher_in,
    out_proj,
    final_gain,
    mean_prev,
    rotation,
    signs,
    prev_scale,
    student_in,
    head_weight,
    image_ids,
):
    rows, own = teacher_in.shape
    part = out_proj.shape[1]
    width = final_gain.shape[0]
    blocks = width // own
    chunks = width // part
    depth = student_in.shape[1] // chunks
    all_tokens = image_ids.shape[0]
    image_count = all_tokens // IMAGE_SHARE
    smem, vmem = pl.BlockSpec(memory_space=pltpu.SMEM), pl.BlockSpec(memory_space=pltpu.VMEM)
    dpos = lax.axis_index(DP)
    tpos = lax.axis_index(TN)
    position = tpos.reshape(1)

    side = dpos % 2
    halves = out_proj.reshape(2, part, part)
    got = []
    for k in range(2):
        send = lax.dynamic_index_in_dim(halves, (side + k) % 2, 0, keepdims=False)
        route = []
        for d in range(chunks):
            for t in range(blocks):
                route.append((d * blocks + t, (2 * t + (d % 2 ^ k)) * blocks + d // 2))
        got.append(lax.ppermute(send, DP + TN, route))
    strip = jnp.where(
        side == 0, jnp.concatenate(got, axis=1), jnp.concatenate(got[::-1], axis=1)
    )
    near = broadcast_gather(strip, "yh")
    teacher = lax.all_gather(teacher_in, TN, axis=0, tiled=False)
    near, teacher = lax.optimization_barrier((near, teacher))
    proj = lax.all_gather(near.reshape(-1, own), "z", axis=0, tiled=True)

    slab = width // lax.axis_size("z")
    few = slab // blocks
    scale = 1.0 / (jnp.sqrt(F32(width)) * prev_scale)
    index_row = lax.broadcasted_iota(jnp.int32, (own, own), 0)
    index_col = lax.broadcasted_iota(jnp.int32, (own, own), 1)
    table = parity_sign(index_row & index_col).astype(BF)
    lines = lax.dynamic_slice_in_dim(rotation, lax.axis_index("z") * slab, slab, 0)
    lines = (lines * (2 * signs - 1).astype(BF)).reshape(blocks, few, own)
    lines = lax.all_to_all(lines, TN, 0, 0, tiled=True)
    lines = pl.pallas_call(
        hadamard_kernel,
        out_shape=jax.ShapeDtypeStruct(lines.shape, BF),
        in_specs=[smem, vmem, vmem],
        out_specs=vmem,
        compiler_params=pltpu.CompilerParams(vmem_limit_bytes=24 << 20),
    )(scale, lines, table)
    lines = lax.all_to_all(lines, TN, 0, 0, tiled=True).reshape(slab, own)

    normed = layer_norm(student_in.astype(F32)).astype(BF)
    predicted = jnp.dot(normed, head_weight, preferred_element_type=F32)
    image_nums = jnp.arange(image_count, dtype=jnp.int32)
    counts = jnp.sum((image_ids[None, :] == image_nums[:, None]).astype(F32), axis=1)
    own_ids = lax.dynamic_slice_in_dim(image_ids, dpos * rows, rows, 0)
    token_counts = jnp.sum(
        jnp.where(own_ids[:, None] == image_nums[None, :], counts[None, :], 0.0), axis=1, keepdims=True
    )
    token_weight = 1.0 / token_counts

    proj, lines, normed, predicted, token_weight = lax.optimization_barrier(
        (proj, lines, normed, predicted, token_weight)
    )
    turned = lax.all_gather(lines, "z", axis=0, tiled=True)
    raw, stat = pl.pallas_call(
        project_kernel,
        out_shape=(jax.ShapeDtypeStruct((rows, own), BF), jax.ShapeDtypeStruct((rows, 2), F32)),
        in_specs=[vmem, vmem],
        out_specs=(vmem, vmem),
        compiler_params=pltpu.CompilerParams(vmem_limit_bytes=40 << 20),
        cost_estimate=pl.CostEstimate(flops=2 * rows * width * own, bytes_accessed=8 << 20, transcendentals=0),
    )(teacher, proj)
    pieces = jnp.stack(split3(stat.T)).reshape(6 * rows // own, own).astype(BF)
    spare = -pieces.shape[0] % 16
    packed = jnp.concatenate([raw, pieces, jnp.zeros((spare, own), BF)])
    mine, other = tensor_gather(packed)
    first = tpos % 2 == 0

    def unpack(block):
        tail = block[:, rows : rows + pieces.shape[0], :].astype(F32)
        return tail.reshape(-1, 3, 2, rows).sum(1)

    stat_mine, stat_other = unpack(mine), jnp.concatenate([unpack(part) for part in other])
    stats = jnp.stack(
        [jnp.where(first, stat_mine, stat_other), jnp.where(first, stat_other, stat_mine)], axis=1
    ).reshape(blocks, 2, rows)
    mean = jnp.mean(stats[:, 0], axis=0)
    adjust = stats[:, 0] - mean
    variance = (jnp.sum(stats[:, 1], axis=0) + own * jnp.sum(adjust * adjust, axis=0)) / width
    rstd = lax.rsqrt(variance + 1e-06)
    adjust = jnp.concatenate([stat_mine[:, 0], stat_other[:, 0]]) - mean

    features, sums = pl.pallas_call(
        feature_kernel,
        out_shape=(
            jax.ShapeDtypeStruct((blocks, rows, own), BF),
            jax.ShapeDtypeStruct((blocks, 1, own), F32),
        ),
        in_specs=[smem] + [vmem] * 6,
        out_specs=(vmem,) * 2,
        compiler_params=pltpu.CompilerParams(vmem_limit_bytes=40 << 20),
        cost_estimate=pl.CostEstimate(flops=rows * width * 8, bytes_accessed=8 << 20, transcendentals=0),
    )(position, mine, *other, adjust.T, rstd[:, None], final_gain.reshape(blocks, 1, own))
    moment = pl.pallas_call(
        moment_kernel,
        out_shape=jax.ShapeDtypeStruct((chunks, own, part), BF),
        in_specs=[smem, vmem, vmem],
        out_specs=vmem,
        compiler_params=pltpu.CompilerParams(vmem_limit_bytes=24 << 20),
        cost_estimate=pl.CostEstimate(flops=2 * rows * width * own, bytes_accessed=6 << 20, transcendentals=0),
    )(position, features, sums)
    within = lax.psum_scatter(moment, "z", scatter_dimension=0, tiled=True)

    sent = pl.pallas_call(
        grad_kernel,
        out_shape=jax.ShapeDtypeStruct((chunks, 2 * depth + 16, part), BF),
        in_specs=[smem] + [vmem] * 7,
        out_specs=vmem,
        compiler_params=pltpu.CompilerParams(vmem_limit_bytes=32 << 20),
        cost_estimate=pl.CostEstimate(flops=3 * rows * width * own, bytes_accessed=9 << 20, transcendentals=0),
    )(position, features, mean_prev.reshape(blocks, 1, own), turned, predicted, token_weight, normed, sums)
    taken = lax.all_to_all(sent, DP, 0, 0, tiled=True)

    grad_own = jnp.sum(taken[:, : 2 * depth, :].astype(F32), axis=0).astype(BF)
    places, here = lax.axis_size("yh"), lax.axis_index("yh")
    within_sum = within[here].astype(F32)
    for k in range(1, places):
        within_sum += shift(within[(here + k) % places], "yh", k).astype(F32)
    grad_head = pl.pallas_call(
        place_kernel,
        out_shape=jax.ShapeDtypeStruct((chunks * depth, own), F32),
        in_specs=[vmem],
        out_specs=vmem,
    )(broadcast_gather(grad_own, DP))

    tail = taken[:, 2 * depth :, :].astype(F32)
    sums_t = tail[:, 0:6].reshape(chunks, 2, 3, part).sum(2).reshape(chunks, own)
    loss = tail[:, 6:12].reshape(chunks, 2, 3, part).sum((0, 2)).reshape(own)
    sums_d = tail[:, 12:15].sum(1)
    new_mean = jnp.sum(sums_t, axis=0) / all_tokens
    mean_d = jnp.sum(sums_d, axis=0) / all_tokens
    off_t = sums_t / rows - new_mean
    off_d = sums_d / rows - mean_d
    between = lax.dot_general(
        off_t, off_d, (((0,), (0,)), ((), ())), precision=lax.Precision.HIGHEST, preferred_element_type=F32
    )
    new_cov = (within_sum + between * rows) / all_tokens
    return (new_cov, new_mean, grad_head, loss / image_count)


def solution(mesh):
    z, y, x = 8, 4, 4
    if mesh.devices.size != 512:
        z, y, x = 2, mesh.shape["dp"] // 2, mesh.shape["tensor"] // 4
    inner = Mesh(mesh.devices.reshape(z, y, x, 2, 2), DP + TN)
    return jax.shard_map(
        body,
        mesh=inner,
        in_specs=(
            P(DP, TN),
            P(TN, DP),
            P(),
            P(),
            P(None, TN),
            P(TN),
            P(),
            P(DP, None),
            P(None, TN),
            P(),
        ),
        out_specs=(P(TN, DP), P(TN), P(None, TN), P(TN)),
        check_vma=False,
    )
```

```python
import jax
import jax.numpy as jnp
from jax import lax
from jax.experimental import pallas as pl
from jax.experimental.pallas import tpu as pltpu
from jax.sharding import Mesh
from jax.sharding import PartitionSpec as P

DP = ("z", "yh")
TN = ("x", "yl", "c")
IMAGE_SHARE = 128
BF = jnp.bfloat16
F32 = jnp.float32


def hold(value):
    return lax.reduce_precision(value, 8, 7)


def split3(value):
    high = hold(value)
    rest = value - high
    mid = hold(rest)
    return high, mid, rest - mid


def broadcast_gather(block, axes):
    count = lax.axis_size(axes)
    return lax.all_to_all(jnp.broadcast_to(block[None], (count,) + block.shape), axes, 0, 0, tiled=True)


def shift(block, axis, step):
    count = lax.axis_size(axis)
    return lax.ppermute(block, axis, [(i, (i + step) % count) for i in range(count)])


def tensor_gather(block):
    mine = broadcast_gather(block, TN[:2])
    return mine, lax.ppermute(mine, "c", [(0, 1), (1, 0)])


def parity_sign(value):
    count = jnp.zeros_like(value)
    for place in range(16):
        count = count + (value >> place & 1)
    return 1 - 2 * (count % 2)


def layer_norm(values):
    centred = values - jnp.mean(values, axis=-1, keepdims=True)
    spread = jnp.mean(centred * centred, axis=-1, keepdims=True)
    return centred * lax.rsqrt(spread + 1e-06)


def project_kernel(x_ref, w_ref, out_ref, stat_ref):
    own = w_ref.shape[1]
    total = jnp.zeros(out_ref.shape, F32)
    for b in range(x_ref.shape[0]):
        total += jnp.dot(x_ref[b], w_ref[b * own : (b + 1) * own, :], preferred_element_type=F32)
    mean = jnp.sum(total, axis=1, keepdims=True) * (1.0 / own)
    centred = total - mean
    out_ref[...] = centred.astype(BF)
    spread = jnp.sum(centred * centred, axis=1, keepdims=True)
    lane = lax.broadcasted_iota(jnp.int32, stat_ref.shape, 1)
    stat_ref[...] = jnp.where(lane == 0, mean, spread)


def feature_kernel(
    pos_ref, mine_ref, other_ref, adj_ref, rstd_ref, gain_ref, prev_ref, turn_ref,
    f_ref, target_ref, sums_ref,
):
    blocks, rows, own = f_ref.shape
    core = lax.rem(pos_ref[0], 2)
    rstd = rstd_ref[...]
    total = jnp.zeros((rows, own), F32)
    for j in range(blocks):
        source, q, side = (mine_ref, j, core) if j < blocks // 2 else (other_ref, j - blocks // 2, 1 - core)
        b = 2 * q + side
        value = (source[q, :rows, :].astype(F32) + adj_ref[:, j : j + 1]) * rstd * gain_ref[b]
        feature = value.astype(BF)
        f_ref[b] = feature
        feature = feature.astype(F32)
        sums_ref[b] = jnp.sum(feature, axis=0, keepdims=True)
        shifted = (feature - prev_ref[b]).astype(BF)
        turn = turn_ref[pl.ds(pl.multiple_of(b * own, own), own), :]
        total += jnp.dot(shifted, turn, preferred_element_type=F32)
    target_ref[...] = total


def moment_kernel(pos_ref, f_ref, sums_ref, out_ref):
    blocks, rows, own = f_ref.shape
    part = out_ref.shape[2]
    own_t = f_ref[pos_ref[0]].astype(F32).T
    own_col = jnp.sum(own_t, axis=1, keepdims=True)
    own_t = own_t.astype(BF)
    for b in range(blocks):
        block = jnp.dot(own_t, f_ref[b], preferred_element_type=F32) - own_col * (sums_ref[b] * (1.0 / rows))
        block = block.astype(BF)
        for h in range(2):
            out_ref[2 * b + h] = block[:, h * part : (h + 1) * part]


def hadamard_kernel(scale_ref, lines_ref, table_ref, out_ref):
    blocks, tall, _ = lines_ref.shape
    few = min(tall, 32)

    def piece(i, _):
        rows = pl.ds(pl.multiple_of(i * few, few), few)
        parts = [
            jnp.dot(lines_ref[b, rows, :], table_ref[...], preferred_element_type=F32) * scale_ref[0]
            for b in range(blocks)
        ]
        step = 1
        while step < blocks:
            parts = [
                parts[b - step] - parts[b] if b & step else parts[b] + parts[b + step] for b in range(blocks)
            ]
            step *= 2
        for b in range(blocks):
            out_ref[b, rows, :] = parts[b].astype(BF)
        return 0

    lax.fori_loop(0, tall // few, piece, 0)


def grad_kernel(pos_ref, target_ref, pred_ref, w_ref, normed_ref, sums_ref, out_ref):
    chunks, _, part = out_ref.shape
    depth = normed_ref.shape[1] // chunks
    residual = pred_ref[...] - target_ref[...]
    weighted = residual * w_ref[...]
    loss = jnp.sum(weighted * residual, axis=0, keepdims=True)
    grad = lax.dot_general(
        normed_ref[...], weighted.astype(BF), (((0,), (0,)), ((), ())), preferred_element_type=F32
    ).astype(BF)
    row = lax.broadcasted_iota(jnp.int32, (16, part), 0)

    def parts(value):
        high = value.astype(BF).astype(F32)
        rest = value - high
        mid = rest.astype(BF).astype(F32)
        return [high, mid, rest - mid]

    own_row = sums_ref[pos_ref[0]]
    fixed = []
    for h in range(2):
        fixed += parts(own_row[:, h * part : (h + 1) * part])
    for h in range(2):
        fixed += parts(loss[:, h * part : (h + 1) * part])
    for d in range(chunks):
        for h in range(2):
            out_ref[d, h * depth : (h + 1) * depth, :] = grad[
                d * depth : (d + 1) * depth, h * part : (h + 1) * part
            ]
        tile = jnp.zeros((16, part), F32)
        here = sums_ref[d // 2][:, (d % 2) * part : (d % 2 + 1) * part]
        for i, piece in enumerate(fixed + parts(here)):
            tile = jnp.where(row == i, piece, tile)
        out_ref[d, 2 * depth :, :] = tile.astype(BF)


def place_kernel(in_ref, out_ref):
    chunks, tall, part = in_ref.shape
    depth = tall // 2
    for d in range(chunks):
        for h in range(2):
            out_ref[d * depth : (d + 1) * depth, h * part : (h + 1) * part] = in_ref[
                d, h * depth : (h + 1) * depth, :
            ].astype(F32)


def body(
    teacher_in,
    out_proj,
    final_gain,
    mean_prev,
    rotation,
    signs,
    prev_scale,
    student_in,
    head_weight,
    image_ids,
):
    rows, own = teacher_in.shape
    part = out_proj.shape[1]
    width = final_gain.shape[0]
    blocks = width // own
    chunks = width // part
    depth = student_in.shape[1] // chunks
    all_tokens = image_ids.shape[0]
    image_count = all_tokens // IMAGE_SHARE
    smem, vmem = pl.BlockSpec(memory_space=pltpu.SMEM), pl.BlockSpec(memory_space=pltpu.VMEM)
    dpos = lax.axis_index(DP)
    tpos = lax.axis_index(TN)
    position = tpos.reshape(1)

    side = dpos % 2
    halves = out_proj.reshape(2, part, part)
    got = []
    for k in range(2):
        send = lax.dynamic_index_in_dim(halves, (side + k) % 2, 0, keepdims=False)
        route = []
        for d in range(chunks):
            for t in range(blocks):
                route.append((d * blocks + t, (2 * t + (d % 2 ^ k)) * blocks + d // 2))
        got.append(lax.ppermute(send, DP + TN, route))
    strip = jnp.where(
        side == 0, jnp.concatenate(got, axis=1), jnp.concatenate(got[::-1], axis=1)
    )
    teacher = lax.all_gather(teacher_in, TN, axis=0, tiled=False)

    scale = 1.0 / (jnp.sqrt(F32(width)) * prev_scale)
    index_row = lax.broadcasted_iota(jnp.int32, (own, own), 0)
    index_col = lax.broadcasted_iota(jnp.int32, (own, own), 1)
    table = parity_sign(index_row & index_col).astype(BF)
    lines = (rotation * (2 * signs - 1).astype(BF)).reshape(blocks, own, own)
    lines = lax.all_to_all(lines, TN, 0, 0, tiled=True)
    strip, lines = lax.optimization_barrier((strip, lines))
    near = broadcast_gather(strip, "yh")
    near, teacher = lax.optimization_barrier((near, teacher))
    proj = lax.all_gather(near.reshape(-1, own), "z", axis=0, tiled=True)
    lines = pl.pallas_call(
        hadamard_kernel,
        out_shape=jax.ShapeDtypeStruct(lines.shape, BF),
        in_specs=[smem, vmem, vmem],
        out_specs=vmem,
        compiler_params=pltpu.CompilerParams(vmem_limit_bytes=16 << 20),
        cost_estimate=pl.CostEstimate(flops=2 * width * own * own, bytes_accessed=4 << 20, transcendentals=0),
    )(scale, lines, table)
    turned = lax.all_to_all(lines, TN, 0, 0, tiled=True).reshape(width, own)

    normed = layer_norm(student_in.astype(F32)).astype(BF)
    predicted = jnp.dot(normed, head_weight, preferred_element_type=F32)
    image_nums = jnp.arange(image_count, dtype=jnp.int32)
    counts = jnp.sum((image_ids[None, :] == image_nums[:, None]).astype(F32), axis=1)
    own_ids = lax.dynamic_slice_in_dim(image_ids, dpos * rows, rows, 0)
    token_counts = jnp.sum(
        jnp.where(own_ids[:, None] == image_nums[None, :], counts[None, :], 0.0), axis=1, keepdims=True
    )
    token_weight = 1.0 / token_counts

    proj, turned, normed, predicted, token_weight = lax.optimization_barrier(
        (proj, turned, normed, predicted, token_weight)
    )
    raw, stat = pl.pallas_call(
        project_kernel,
        out_shape=(jax.ShapeDtypeStruct((rows, own), BF), jax.ShapeDtypeStruct((rows, 2), F32)),
        in_specs=[vmem, vmem],
        out_specs=(vmem, vmem),
        compiler_params=pltpu.CompilerParams(vmem_limit_bytes=16 << 20),
        cost_estimate=pl.CostEstimate(flops=2 * rows * width * own, bytes_accessed=8 << 20, transcendentals=0),
    )(teacher, proj)
    pieces = jnp.stack(split3(stat.T)).reshape(6 * rows // own, own).astype(BF)
    spare = -pieces.shape[0] % 16
    packed = jnp.concatenate([raw, pieces, jnp.zeros((spare, own), BF)])
    mine, other = tensor_gather(packed)
    first = tpos % 2 == 0

    def unpack(block):
        tail = block[:, rows : rows + pieces.shape[0], :].astype(F32)
        return tail.reshape(blocks // 2, 3, 2, rows).sum(1)

    stat_mine, stat_other = unpack(mine), unpack(other)
    stats = jnp.stack(
        [jnp.where(first, stat_mine, stat_other), jnp.where(first, stat_other, stat_mine)], axis=1
    ).reshape(blocks, 2, rows)
    mean = jnp.mean(stats[:, 0], axis=0)
    adjust = stats[:, 0] - mean
    variance = (jnp.sum(stats[:, 1], axis=0) + own * jnp.sum(adjust * adjust, axis=0)) / width
    rstd = lax.rsqrt(variance + 1e-06)
    adjust = jnp.concatenate([stat_mine[:, 0], stat_other[:, 0]]) - mean

    features, target, sums = pl.pallas_call(
        feature_kernel,
        out_shape=(
            jax.ShapeDtypeStruct((blocks, rows, own), BF),
            jax.ShapeDtypeStruct((rows, own), F32),
            jax.ShapeDtypeStruct((blocks, 1, own), F32),
        ),
        in_specs=[smem] + [vmem] * 7,
        out_specs=(vmem,) * 3,
        compiler_params=pltpu.CompilerParams(vmem_limit_bytes=16 << 20),
        cost_estimate=pl.CostEstimate(flops=2 * rows * width * own, bytes_accessed=12 << 20, transcendentals=0),
    )(
        position,
        mine,
        other,
        adjust.T,
        rstd[:, None],
        final_gain.reshape(blocks, 1, own),
        mean_prev.reshape(blocks, 1, own),
        turned,
    )
    moment = pl.pallas_call(
        moment_kernel,
        out_shape=jax.ShapeDtypeStruct((chunks, own, part), BF),
        in_specs=[smem, vmem, vmem],
        out_specs=vmem,
        compiler_params=pltpu.CompilerParams(vmem_limit_bytes=16 << 20),
        cost_estimate=pl.CostEstimate(flops=2 * rows * width * own, bytes_accessed=6 << 20, transcendentals=0),
    )(position, features, sums)
    within = lax.psum_scatter(moment, "z", scatter_dimension=0, tiled=True)

    sent = pl.pallas_call(
        grad_kernel,
        out_shape=jax.ShapeDtypeStruct((chunks, 2 * depth + 16, part), BF),
        in_specs=[smem] + [vmem] * 5,
        out_specs=vmem,
        compiler_params=pltpu.CompilerParams(vmem_limit_bytes=16 << 20),
    )(position, target, predicted, token_weight, normed, sums)
    taken = lax.all_to_all(sent, DP, 0, 0, tiled=True)

    grad_own = jnp.sum(taken[:, : 2 * depth, :].astype(F32), axis=0).astype(BF)
    places, here = lax.axis_size("yh"), lax.axis_index("yh")
    within_sum = within[here].astype(F32)
    for k in range(1, places):
        within_sum += shift(within[(here + k) % places], "yh", k).astype(F32)
    grad_head = pl.pallas_call(
        place_kernel,
        out_shape=jax.ShapeDtypeStruct((chunks * depth, own), F32),
        in_specs=[vmem],
        out_specs=vmem,
    )(broadcast_gather(grad_own, DP))

    tail = taken[:, 2 * depth :, :].astype(F32)
    sums_t = tail[:, 0:6].reshape(chunks, 2, 3, part).sum(2).reshape(chunks, own)
    loss = tail[:, 6:12].reshape(chunks, 2, 3, part).sum((0, 2)).reshape(own)
    sums_d = tail[:, 12:15].sum(1)
    new_mean = jnp.sum(sums_t, axis=0) / all_tokens
    mean_d = jnp.sum(sums_d, axis=0) / all_tokens
    off_t = sums_t / rows - new_mean
    off_d = sums_d / rows - mean_d
    between = lax.dot_general(
        off_t, off_d, (((0,), (0,)), ((), ())), precision=lax.Precision.HIGHEST, preferred_element_type=F32
    )
    new_cov = (within_sum + between * rows) / all_tokens
    return (new_cov, new_mean, grad_head, loss / image_count)


def solution(mesh):
    z, y, x = 8, 4, 4
    if mesh.devices.size != 512:
        z, y, x = 2, mesh.shape["dp"] // 2, mesh.shape["tensor"] // 4
    inner = Mesh(mesh.devices.reshape(z, y, x, 2, 2), DP + TN)
    return jax.shard_map(
        body,
        mesh=inner,
        in_specs=(
            P(DP, TN),
            P(TN, DP),
            P(),
            P(),
            P(None, TN),
            P(TN),
            P(),
            P(DP, None),
            P(None, TN),
            P(),
        ),
        out_specs=(P(TN, DP), P(TN), P(None, TN), P(TN)),
        check_vma=False,
    )
```

```python
import jax
import jax.numpy as jnp
from jax import lax
from jax.experimental import pallas as pl
from jax.experimental.pallas import tpu as pltpu
from jax.sharding import Mesh
from jax.sharding import PartitionSpec as P

DP = ("z", "yh")
TN = ("x", "yl", "c")
IMAGE_SHARE = 128
BF = jnp.bfloat16
F32 = jnp.float32


def hold(value):
    return lax.reduce_precision(value, 8, 7)


def split3(value):
    high = hold(value)
    rest = value - high
    mid = hold(rest)
    return high, mid, rest - mid


def broadcast_gather(block, axes):
    count = lax.axis_size(axes)
    return lax.all_to_all(jnp.broadcast_to(block[None], (count,) + block.shape), axes, 0, 0, tiled=True)


def shift(block, axis, step):
    count = lax.axis_size(axis)
    return lax.ppermute(block, axis, [(i, (i + step) % count) for i in range(count)])


def tensor_gather(block):
    mine = broadcast_gather(block, TN[:2])
    return mine, lax.ppermute(mine, "c", [(0, 1), (1, 0)])


def tensor_gather_twice(block):
    other = lax.ppermute(block, "c", [(0, 1), (1, 0)])
    return broadcast_gather(block, TN[:2]), broadcast_gather(other, TN[:2])


def parity_sign(value):
    count = jnp.zeros_like(value)
    for place in range(16):
        count = count + (value >> place & 1)
    return 1 - 2 * (count % 2)


def layer_norm(values):
    centred = values - jnp.mean(values, axis=-1, keepdims=True)
    spread = jnp.mean(centred * centred, axis=-1, keepdims=True)
    return centred * lax.rsqrt(spread + 1e-06)


def project_kernel(pos_ref, mine_ref, other_ref, w_ref, out_ref, stat_ref):
    own = w_ref.shape[1]
    core = lax.rem(pos_ref[0], 2)
    total = jnp.zeros(out_ref.shape, F32)
    for source, side in ((mine_ref, core), (other_ref, 1 - core)):
        for q in range(source.shape[0]):
            start = pl.multiple_of((2 * q + side) * own, own)
            total += jnp.dot(source[q], w_ref[pl.ds(start, own), :], preferred_element_type=F32)
    mean = jnp.sum(total, axis=1, keepdims=True) * (1.0 / own)
    centred = total - mean
    out_ref[...] = centred.astype(BF)
    spread = jnp.sum(centred * centred, axis=1, keepdims=True)
    lane = lax.broadcasted_iota(jnp.int32, stat_ref.shape, 1)
    stat_ref[...] = jnp.where(lane == 0, mean, spread)


def feature_kernel(
    pos_ref, mine_ref, other_ref, adj_ref, rstd_ref, gain_ref, prev_ref, rot_ref, sign_ref,
    f_ref, basis_ref, sums_ref,
):
    blocks, rows, own = f_ref.shape
    core = lax.rem(pos_ref[0], 2)
    rstd = rstd_ref[...]
    total = jnp.zeros((rows, own), F32)
    for j in range(blocks):
        source, q, side = (mine_ref, j, core) if j < blocks // 2 else (other_ref, j - blocks // 2, 1 - core)
        b = 2 * q + side
        value = (source[q, :rows, :].astype(F32) + adj_ref[:, j : j + 1]) * rstd * gain_ref[b]
        feature = value.astype(BF)
        f_ref[b] = feature
        feature = feature.astype(F32)
        sums_ref[b] = jnp.sum(feature, axis=0, keepdims=True)
        shifted = (feature - prev_ref[b]).astype(BF)
        turn = rot_ref[pl.ds(pl.multiple_of(b * own, own), own), :]
        total += jnp.dot(shifted, turn, preferred_element_type=F32)
    basis_ref[...] = total.astype(BF) * sign_ref[...]


def moment_kernel(pos_ref, f_ref, sums_ref, out_ref):
    blocks, rows, own = f_ref.shape
    part = out_ref.shape[2]
    own_t = f_ref[pos_ref[0]].astype(F32).T
    own_col = jnp.sum(own_t, axis=1, keepdims=True)
    own_t = own_t.astype(BF)
    for b in range(blocks):
        block = jnp.dot(own_t, f_ref[b], preferred_element_type=F32) - own_col * (sums_ref[b] * (1.0 / rows))
        block = block.astype(BF)
        for h in range(2):
            out_ref[2 * b + h] = block[:, h * part : (h + 1) * part]


def hadamard_kernel(scale_ref, basis_ref, table_ref, out_ref):
    blocks, few, own = basis_ref.shape
    flat = basis_ref[...].reshape(blocks * few, own)
    mixed = jnp.dot(flat, table_ref[...], preferred_element_type=F32) * scale_ref[0]
    parts = [mixed[b * few : (b + 1) * few] for b in range(blocks)]
    step = 1
    while step < blocks:
        parts = [
            parts[b - step] - parts[b] if b & step else parts[b] + parts[b + step] for b in range(blocks)
        ]
        step *= 2
    for b in range(blocks):
        out_ref[b] = parts[b].astype(BF)


def grad_kernel(pos_ref, target_ref, pred_ref, w_ref, normed_ref, sums_ref, out_ref):
    chunks, _, part = out_ref.shape
    depth = normed_ref.shape[1] // chunks
    residual = pred_ref[...] - target_ref[...].astype(F32)
    weighted = residual * w_ref[...]
    loss = jnp.sum(weighted * residual, axis=0, keepdims=True)
    grad = lax.dot_general(
        normed_ref[...], weighted.astype(BF), (((0,), (0,)), ((), ())), preferred_element_type=F32
    ).astype(BF)
    row = lax.broadcasted_iota(jnp.int32, (16, part), 0)

    def parts(value):
        high = value.astype(BF).astype(F32)
        rest = value - high
        mid = rest.astype(BF).astype(F32)
        return [high, mid, rest - mid]

    own_row = sums_ref[pos_ref[0]]
    fixed = []
    for h in range(2):
        fixed += parts(own_row[:, h * part : (h + 1) * part])
    for h in range(2):
        fixed += parts(loss[:, h * part : (h + 1) * part])
    for d in range(chunks):
        for h in range(2):
            out_ref[d, h * depth : (h + 1) * depth, :] = grad[
                d * depth : (d + 1) * depth, h * part : (h + 1) * part
            ]
        tile = jnp.zeros((16, part), F32)
        here = sums_ref[d // 2][:, (d % 2) * part : (d % 2 + 1) * part]
        for i, piece in enumerate(fixed + parts(here)):
            tile = jnp.where(row == i, piece, tile)
        out_ref[d, 2 * depth :, :] = tile.astype(BF)


def place_kernel(in_ref, out_ref):
    chunks, tall, part = in_ref.shape
    depth = tall // 2
    for d in range(chunks):
        for h in range(2):
            out_ref[d * depth : (d + 1) * depth, h * part : (h + 1) * part] = in_ref[
                d, h * depth : (h + 1) * depth, :
            ].astype(F32)


def body(
    teacher_in,
    out_proj,
    final_gain,
    mean_prev,
    rotation,
    signs,
    prev_scale,
    student_in,
    head_weight,
    image_ids,
):
    rows, own = teacher_in.shape
    part = out_proj.shape[1]
    width = final_gain.shape[0]
    blocks = width // own
    chunks = width // part
    depth = student_in.shape[1] // chunks
    all_tokens = image_ids.shape[0]
    image_count = all_tokens // IMAGE_SHARE
    dpos = lax.axis_index(DP)
    tpos = lax.axis_index(TN)

    side = dpos % 2
    halves = out_proj.reshape(2, part, part)
    got = []
    for k in range(2):
        send = lax.dynamic_index_in_dim(halves, (side + k) % 2, 0, keepdims=False)
        route = []
        for d in range(chunks):
            for t in range(blocks):
                route.append((d * blocks + t, (2 * t + (d % 2 ^ k)) * blocks + d // 2))
        got.append(lax.ppermute(send, DP + TN, route))
    strip = jnp.where(
        side == 0, jnp.concatenate(got, axis=1), jnp.concatenate(got[::-1], axis=1)
    )
    near = broadcast_gather(strip, "yh")
    proj = lax.all_gather(near.reshape(-1, own), "z", axis=0, tiled=True)
    teacher, _ = lax.optimization_barrier((teacher_in, near))
    teacher = lax.cond(image_ids[0] >= 0, tensor_gather, tensor_gather_twice, teacher)

    normed = layer_norm(student_in.astype(F32)).astype(BF)
    predicted = jnp.dot(normed, head_weight, preferred_element_type=F32)
    image_nums = jnp.arange(image_count, dtype=jnp.int32)
    counts = jnp.sum((image_ids[None, :] == image_nums[:, None]).astype(F32), axis=1)
    own_ids = lax.dynamic_slice_in_dim(image_ids, dpos * rows, rows, 0)
    token_counts = jnp.sum(
        jnp.where(own_ids[:, None] == image_nums[None, :], counts[None, :], 0.0), axis=1, keepdims=True
    )
    token_weight = 1.0 / token_counts

    smem, vmem = pl.BlockSpec(memory_space=pltpu.SMEM), pl.BlockSpec(memory_space=pltpu.VMEM)
    position = tpos.reshape(1)
    proj, normed, predicted, token_weight = lax.optimization_barrier((proj, normed, predicted, token_weight))
    raw, stat = pl.pallas_call(
        project_kernel,
        out_shape=(jax.ShapeDtypeStruct((rows, own), BF), jax.ShapeDtypeStruct((rows, 2), F32)),
        in_specs=[smem, vmem, vmem, vmem],
        out_specs=(vmem, vmem),
        compiler_params=pltpu.CompilerParams(vmem_limit_bytes=16 << 20),
        cost_estimate=pl.CostEstimate(flops=2 * rows * width * own, bytes_accessed=8 << 20, transcendentals=0),
    )(position, *teacher, proj)
    pieces = jnp.stack(split3(stat.T)).reshape(6 * rows // own, own).astype(BF)
    spare = -pieces.shape[0] % 16
    packed = jnp.concatenate([raw, pieces, jnp.zeros((spare, own), BF)])
    mine, other = tensor_gather(packed)
    first = tpos % 2 == 0

    def unpack(block):
        tail = block[:, rows : rows + pieces.shape[0], :].astype(F32)
        return tail.reshape(blocks // 2, 3, 2, rows).sum(1)

    stat_mine, stat_other = unpack(mine), unpack(other)
    stats = jnp.stack(
        [jnp.where(first, stat_mine, stat_other), jnp.where(first, stat_other, stat_mine)], axis=1
    ).reshape(blocks, 2, rows)
    mean = jnp.mean(stats[:, 0], axis=0)
    adjust = stats[:, 0] - mean
    variance = (jnp.sum(stats[:, 1], axis=0) + own * jnp.sum(adjust * adjust, axis=0)) / width
    rstd = lax.rsqrt(variance + 1e-06)
    adjust = jnp.concatenate([stat_mine[:, 0], stat_other[:, 0]]) - mean
    scale = 1.0 / (jnp.sqrt(F32(width)) * prev_scale)
    index_row = lax.broadcasted_iota(jnp.int32, (own, own), 0)
    index_col = lax.broadcasted_iota(jnp.int32, (own, own), 1)
    table = parity_sign(index_row & index_col).astype(BF)

    features, basis, sums = pl.pallas_call(
        feature_kernel,
        out_shape=(
            jax.ShapeDtypeStruct((blocks, rows, own), BF),
            jax.ShapeDtypeStruct((rows, own), BF),
            jax.ShapeDtypeStruct((blocks, 1, own), F32),
        ),
        in_specs=[smem] + [vmem] * 8,
        out_specs=(vmem,) * 3,
        compiler_params=pltpu.CompilerParams(vmem_limit_bytes=16 << 20),
        cost_estimate=pl.CostEstimate(flops=2 * rows * width * own, bytes_accessed=12 << 20, transcendentals=0),
    )(
        position,
        mine,
        other,
        adjust.T,
        rstd[:, None],
        final_gain.reshape(blocks, 1, own),
        mean_prev.reshape(blocks, 1, own),
        rotation,
        (2 * signs - 1).astype(BF)[None, :],
    )
    lines = lax.all_to_all(basis.reshape(blocks, rows // blocks, own), TN, 0, 0, tiled=True)
    moment = pl.pallas_call(
        moment_kernel,
        out_shape=jax.ShapeDtypeStruct((chunks, own, part), BF),
        in_specs=[smem, vmem, vmem],
        out_specs=vmem,
        compiler_params=pltpu.CompilerParams(vmem_limit_bytes=12 << 20),
        cost_estimate=pl.CostEstimate(flops=2 * rows * width * own, bytes_accessed=6 << 20, transcendentals=0),
    )(position, features, sums)
    within = lax.psum_scatter(moment, "z", scatter_dimension=0, tiled=True)

    lines = pl.pallas_call(
        hadamard_kernel,
        out_shape=jax.ShapeDtypeStruct(lines.shape, BF),
        in_specs=[smem, vmem, vmem],
        out_specs=vmem,
        compiler_params=pltpu.CompilerParams(vmem_limit_bytes=12 << 20),
    )(scale, lines, table)
    target = lax.all_to_all(lines, TN, 0, 0, tiled=True).reshape(rows, own)

    sent = pl.pallas_call(
        grad_kernel,
        out_shape=jax.ShapeDtypeStruct((chunks, 2 * depth + 16, part), BF),
        in_specs=[smem] + [vmem] * 5,
        out_specs=vmem,
        compiler_params=pltpu.CompilerParams(vmem_limit_bytes=12 << 20),
    )(position, target, predicted, token_weight, normed, sums)
    taken = lax.all_to_all(sent, DP, 0, 0, tiled=True)

    grad_own = jnp.sum(taken[:, : 2 * depth, :].astype(F32), axis=0).astype(BF)
    places, here = lax.axis_size("yh"), lax.axis_index("yh")
    within_sum = within[here].astype(F32)
    for k in range(1, places):
        within_sum += shift(within[(here + k) % places], "yh", k).astype(F32)
    grad_head = pl.pallas_call(
        place_kernel,
        out_shape=jax.ShapeDtypeStruct((chunks * depth, own), F32),
        in_specs=[vmem],
        out_specs=vmem,
    )(broadcast_gather(grad_own, DP))

    tail = taken[:, 2 * depth :, :].astype(F32)
    sums_t = tail[:, 0:6].reshape(chunks, 2, 3, part).sum(2).reshape(chunks, own)
    loss = tail[:, 6:12].reshape(chunks, 2, 3, part).sum((0, 2)).reshape(own)
    sums_d = tail[:, 12:15].sum(1)
    new_mean = jnp.sum(sums_t, axis=0) / all_tokens
    mean_d = jnp.sum(sums_d, axis=0) / all_tokens
    off_t = sums_t / rows - new_mean
    off_d = sums_d / rows - mean_d
    between = lax.dot_general(
        off_t, off_d, (((0,), (0,)), ((), ())), precision=lax.Precision.HIGHEST, preferred_element_type=F32
    )
    new_cov = (within_sum + between * rows) / all_tokens
    return (new_cov, new_mean, grad_head, loss / image_count)


def solution(mesh):
    z, y, x = 8, 4, 4
    if mesh.devices.size != 512:
        z, y, x = 2, mesh.shape["dp"] // 2, mesh.shape["tensor"] // 4
    inner = Mesh(mesh.devices.reshape(z, y, x, 2, 2), DP + TN)
    return jax.shard_map(
        body,
        mesh=inner,
        in_specs=(
            P(DP, TN),
            P(TN, DP),
            P(),
            P(),
            P(None, TN),
            P(TN),
            P(),
            P(DP, None),
            P(None, TN),
            P(),
        ),
        out_specs=(P(TN, DP), P(TN), P(None, TN), P(TN)),
        check_vma=False,
    )
```

```python
import jax
import jax.numpy as jnp
from jax import lax
from jax.experimental import pallas as pl
from jax.experimental.pallas import tpu as pltpu
from jax.sharding import Mesh
from jax.sharding import PartitionSpec as P

DP = ("z", "yh")
TN = ("x", "yl", "c")
IMAGE_SHARE = 128
BF = jnp.bfloat16
F32 = jnp.float32


def hold(value):
    return lax.reduce_precision(value, 8, 7)


def split3(value):
    high = hold(value)
    rest = value - high
    mid = hold(rest)
    return high, mid, rest - mid


def broadcast_gather(block, axes):
    count = lax.axis_size(axes)
    return lax.all_to_all(jnp.broadcast_to(block[None], (count,) + block.shape), axes, 0, 0, tiled=True)


def shift(block, axis, step):
    count = lax.axis_size(axis)
    return lax.ppermute(block, axis, [(i, (i + step) % count) for i in range(count)])


def tensor_gather(block):
    mine = broadcast_gather(block, TN[:2])
    return mine, lax.ppermute(mine, "c", [(0, 1), (1, 0)])


def tensor_gather_twice(block):
    other = lax.ppermute(block, "c", [(0, 1), (1, 0)])
    return broadcast_gather(block, TN[:2]), broadcast_gather(other, TN[:2])


def parity_sign(value):
    count = jnp.zeros_like(value)
    for place in range(16):
        count = count + (value >> place & 1)
    return 1 - 2 * (count % 2)


def layer_norm(values):
    centred = values - jnp.mean(values, axis=-1, keepdims=True)
    spread = jnp.mean(centred * centred, axis=-1, keepdims=True)
    return centred * lax.rsqrt(spread + 1e-06)


def fetch(copies):
    for copy in copies:
        copy.start()
    return copies


def project_kernel(pos_ref, mine_hbm, other_hbm, w_hbm, out_ref, stat_ref, x_ref, w_ref, x_sem, w_sem):
    count, own = x_ref.shape[0], x_ref.shape[2]
    core = lax.rem(pos_ref[0], 2)
    order = [(mine_hbm, q, 2 * q + core) for q in range(count // 2)]
    order += [(other_hbm, q, 2 * q + 1 - core) for q in range(count // 2)]
    x_copies, w_copies = [], []
    for j, (source, q, b) in enumerate(order):
        x_copies += fetch([pltpu.make_async_copy(source.at[q], x_ref.at[j], x_sem.at[j])])
        w_copies += fetch([pltpu.make_async_copy(w_hbm.at[b], w_ref.at[j], w_sem.at[j])])
    total = jnp.zeros(out_ref.shape, F32)
    for j in range(count):
        x_copies[j].wait()
        w_copies[j].wait()
        total += jnp.dot(x_ref[j], w_ref[j], preferred_element_type=F32)
    mean = jnp.sum(total, axis=1, keepdims=True) * (1.0 / own)
    centred = total - mean
    out_ref[...] = centred.astype(BF)
    spread = jnp.sum(centred * centred, axis=1, keepdims=True)
    lane = lax.broadcasted_iota(jnp.int32, stat_ref.shape, 1)
    stat_ref[...] = jnp.where(lane == 0, mean, spread)


def feature_kernel(
    pos_ref, mine_hbm, other_hbm, adj_ref, rstd_ref, gain_ref, prev_ref, rot_hbm, sign_ref,
    out_ref, basis_ref, sums_ref, f_ref, x_ref, rot_ref, x_sem, rot_sem,
):
    blocks, rows, own = f_ref.shape
    core = lax.rem(pos_ref[0], 2)
    order = [(mine_hbm, q, 2 * q + core) for q in range(blocks // 2)]
    order += [(other_hbm, q, 2 * q + 1 - core) for q in range(blocks // 2)]
    x_copies, rot_copies = [], []
    for j, (source, q, b) in enumerate(order):
        x_copies += fetch([pltpu.make_async_copy(source.at[q], x_ref.at[j], x_sem.at[j])])
        rot_copies += fetch([pltpu.make_async_copy(rot_hbm.at[b], rot_ref.at[j], rot_sem.at[j])])
    rstd = rstd_ref[...]
    total = jnp.zeros((rows, own), F32)
    for j, (_, _, b) in enumerate(order):
        x_copies[j].wait()
        value = (x_ref[j, :rows, :].astype(F32) + adj_ref[:, j : j + 1]) * rstd * gain_ref[b]
        feature = value.astype(BF)
        f_ref[b] = feature
        feature = feature.astype(F32)
        sums_ref[b] = jnp.sum(feature, axis=0, keepdims=True)
        shifted = (feature - prev_ref[b]).astype(BF)
        rot_copies[j].wait()
        total += jnp.dot(shifted, rot_ref[j], preferred_element_type=F32)
    basis_ref[...] = total.astype(BF) * sign_ref[...]
    part = out_ref.shape[2]
    own_t = f_ref[pos_ref[0]].astype(F32).T
    own_col = jnp.sum(own_t, axis=1, keepdims=True)
    own_t = own_t.astype(BF)
    for b in range(blocks):
        block = jnp.dot(own_t, f_ref[b], preferred_element_type=F32) - own_col * (sums_ref[b] * (1.0 / rows))
        block = block.astype(BF)
        for h in range(2):
            out_ref[2 * b + h] = block[:, h * part : (h + 1) * part]


def hadamard_kernel(scale_ref, basis_ref, table_ref, out_ref):
    blocks, few, own = basis_ref.shape
    flat = basis_ref[...].reshape(blocks * few, own)
    mixed = jnp.dot(flat, table_ref[...], preferred_element_type=F32) * scale_ref[0]
    parts = [mixed[b * few : (b + 1) * few] for b in range(blocks)]
    step = 1
    while step < blocks:
        parts = [
            parts[b - step] - parts[b] if b & step else parts[b] + parts[b + step] for b in range(blocks)
        ]
        step *= 2
    for b in range(blocks):
        out_ref[b] = parts[b].astype(BF)


def grad_kernel(pos_ref, target_ref, pred_ref, w_ref, normed_ref, sums_ref, out_ref):
    chunks, _, part = out_ref.shape
    depth = normed_ref.shape[1] // chunks
    residual = pred_ref[...] - target_ref[...].astype(F32)
    weighted = residual * w_ref[...]
    loss = jnp.sum(weighted * residual, axis=0, keepdims=True)
    grad = lax.dot_general(
        normed_ref[...], weighted.astype(BF), (((0,), (0,)), ((), ())), preferred_element_type=F32
    ).astype(BF)
    row = lax.broadcasted_iota(jnp.int32, (16, part), 0)

    def parts(value):
        high = value.astype(BF).astype(F32)
        rest = value - high
        mid = rest.astype(BF).astype(F32)
        return [high, mid, rest - mid]

    own_row = sums_ref[pos_ref[0]]
    fixed = []
    for h in range(2):
        fixed += parts(own_row[:, h * part : (h + 1) * part])
    for h in range(2):
        fixed += parts(loss[:, h * part : (h + 1) * part])
    for d in range(chunks):
        for h in range(2):
            out_ref[d, h * depth : (h + 1) * depth, :] = grad[
                d * depth : (d + 1) * depth, h * part : (h + 1) * part
            ]
        tile = jnp.zeros((16, part), F32)
        here = sums_ref[d // 2][:, (d % 2) * part : (d % 2 + 1) * part]
        for i, piece in enumerate(fixed + parts(here)):
            tile = jnp.where(row == i, piece, tile)
        out_ref[d, 2 * depth :, :] = tile.astype(BF)


def place_kernel(in_ref, out_ref):
    chunks, tall, part = in_ref.shape
    depth = tall // 2
    for d in range(chunks):
        for h in range(2):
            out_ref[d * depth : (d + 1) * depth, h * part : (h + 1) * part] = in_ref[
                d, h * depth : (h + 1) * depth, :
            ].astype(F32)


def body(
    teacher_in,
    out_proj,
    final_gain,
    mean_prev,
    rotation,
    signs,
    prev_scale,
    student_in,
    head_weight,
    image_ids,
):
    rows, own = teacher_in.shape
    part = out_proj.shape[1]
    width = final_gain.shape[0]
    blocks = width // own
    chunks = width // part
    depth = student_in.shape[1] // chunks
    all_tokens = image_ids.shape[0]
    image_count = all_tokens // IMAGE_SHARE
    dpos = lax.axis_index(DP)
    tpos = lax.axis_index(TN)

    side = dpos % 2
    halves = out_proj.reshape(2, part, part)
    got = []
    for k in range(2):
        send = lax.dynamic_index_in_dim(halves, (side + k) % 2, 0, keepdims=False)
        route = []
        for d in range(chunks):
            for t in range(blocks):
                route.append((d * blocks + t, (2 * t + (d % 2 ^ k)) * blocks + d // 2))
        got.append(lax.ppermute(send, DP + TN, route))
    strip = jnp.where(
        side == 0, jnp.concatenate(got, axis=1), jnp.concatenate(got[::-1], axis=1)
    )
    near = broadcast_gather(strip, "yh")
    proj = lax.all_gather(near.reshape(-1, own), "z", axis=0, tiled=True)
    teacher, _ = lax.optimization_barrier((teacher_in, near))
    teacher = lax.cond(prev_scale[0] > 0.0, tensor_gather, tensor_gather_twice, teacher)

    normed = layer_norm(student_in.astype(F32)).astype(BF)
    predicted = jnp.dot(normed, head_weight, preferred_element_type=F32)
    image_nums = jnp.arange(image_count, dtype=jnp.int32)
    counts = jnp.sum((image_ids[None, :] == image_nums[:, None]).astype(F32), axis=1)
    own_ids = lax.dynamic_slice_in_dim(image_ids, dpos * rows, rows, 0)
    token_counts = jnp.sum(
        jnp.where(own_ids[:, None] == image_nums[None, :], counts[None, :], 0.0), axis=1, keepdims=True
    )
    token_weight = 1.0 / token_counts

    smem, vmem = pl.BlockSpec(memory_space=pltpu.SMEM), pl.BlockSpec(memory_space=pltpu.VMEM)
    anywhere = pl.BlockSpec(memory_space=pl.ANY)
    position = tpos.reshape(1)
    raw, stat = pl.pallas_call(
        project_kernel,
        out_shape=(jax.ShapeDtypeStruct((rows, own), BF), jax.ShapeDtypeStruct((rows, 2), F32)),
        in_specs=[smem] + [anywhere] * 3,
        out_specs=(vmem, vmem),
        scratch_shapes=[
            pltpu.VMEM((blocks, rows, own), BF),
            pltpu.VMEM((blocks, own, own), BF),
            pltpu.SemaphoreType.DMA((blocks,)),
            pltpu.SemaphoreType.DMA((blocks,)),
        ],
        compiler_params=pltpu.CompilerParams(vmem_limit_bytes=52 << 20),
        cost_estimate=pl.CostEstimate(flops=2 * rows * width * own, bytes_accessed=8 << 20, transcendentals=0),
    )(position, *teacher, proj.reshape(blocks, own, own))
    pieces = jnp.stack(split3(stat.T)).reshape(6 * rows // own, own).astype(BF)
    spare = -pieces.shape[0] % 16
    packed = jnp.concatenate([raw, pieces, jnp.zeros((spare, own), BF)])
    mine, other = tensor_gather(packed)
    first = tpos % 2 == 0

    def unpack(block):
        tail = block[:, rows : rows + pieces.shape[0], :].astype(F32)
        return tail.reshape(blocks // 2, 3, 2, rows).sum(1)

    stat_mine, stat_other = unpack(mine), unpack(other)
    stats = jnp.stack(
        [jnp.where(first, stat_mine, stat_other), jnp.where(first, stat_other, stat_mine)], axis=1
    ).reshape(blocks, 2, rows)
    mean = jnp.mean(stats[:, 0], axis=0)
    adjust = stats[:, 0] - mean
    variance = (jnp.sum(stats[:, 1], axis=0) + own * jnp.sum(adjust * adjust, axis=0)) / width
    rstd = lax.rsqrt(variance + 1e-06)
    adjust = jnp.concatenate([stat_mine[:, 0], stat_other[:, 0]]) - mean
    scale = 1.0 / (jnp.sqrt(F32(width)) * prev_scale)
    index_row = lax.broadcasted_iota(jnp.int32, (own, own), 0)
    index_col = lax.broadcasted_iota(jnp.int32, (own, own), 1)
    table = parity_sign(index_row & index_col).astype(BF)

    moment, basis, sums = pl.pallas_call(
        feature_kernel,
        out_shape=(
            jax.ShapeDtypeStruct((chunks, own, part), BF),
            jax.ShapeDtypeStruct((rows, own), BF),
            jax.ShapeDtypeStruct((blocks, 1, own), F32),
        ),
        in_specs=[smem, anywhere, anywhere, vmem, vmem, vmem, vmem, anywhere, vmem],
        out_specs=(vmem,) * 3,
        scratch_shapes=[
            pltpu.VMEM((blocks, rows, own), BF),
            pltpu.VMEM((blocks,) + packed.shape, BF),
            pltpu.VMEM((blocks, own, own), BF),
            pltpu.SemaphoreType.DMA((blocks,)),
            pltpu.SemaphoreType.DMA((blocks,)),
        ],
        compiler_params=pltpu.CompilerParams(vmem_limit_bytes=52 << 20),
        cost_estimate=pl.CostEstimate(flops=4 * rows * width * own, bytes_accessed=12 << 20, transcendentals=0),
    )(
        position,
        mine,
        other,
        adjust.T,
        rstd[:, None],
        final_gain.reshape(blocks, 1, own),
        mean_prev.reshape(blocks, 1, own),
        rotation.reshape(blocks, own, own),
        (2 * signs - 1).astype(BF)[None, :],
    )
    lines = lax.all_to_all(basis.reshape(blocks, rows // blocks, own), TN, 0, 0, tiled=True)
    within = lax.psum_scatter(moment, "z", scatter_dimension=0, tiled=True)

    lines = pl.pallas_call(
        hadamard_kernel,
        out_shape=jax.ShapeDtypeStruct(lines.shape, BF),
        in_specs=[smem, vmem, vmem],
        out_specs=vmem,
        compiler_params=pltpu.CompilerParams(vmem_limit_bytes=12 << 20),
    )(scale, lines, table)
    target = lax.all_to_all(lines, TN, 0, 0, tiled=True).reshape(rows, own)

    sent = pl.pallas_call(
        grad_kernel,
        out_shape=jax.ShapeDtypeStruct((chunks, 2 * depth + 16, part), BF),
        in_specs=[smem] + [vmem] * 5,
        out_specs=vmem,
        compiler_params=pltpu.CompilerParams(vmem_limit_bytes=12 << 20),
    )(position, target, predicted, token_weight, normed, sums)
    taken = lax.all_to_all(sent, DP, 0, 0, tiled=True)

    grad_own = jnp.sum(taken[:, : 2 * depth, :].astype(F32), axis=0).astype(BF)
    places, here = lax.axis_size("yh"), lax.axis_index("yh")
    within_sum = within[here].astype(F32)
    for k in range(1, places):
        within_sum += shift(within[(here + k) % places], "yh", k).astype(F32)
    grad_head = pl.pallas_call(
        place_kernel,
        out_shape=jax.ShapeDtypeStruct((chunks * depth, own), F32),
        in_specs=[vmem],
        out_specs=vmem,
    )(broadcast_gather(grad_own, DP))

    tail = taken[:, 2 * depth :, :].astype(F32)
    sums_t = tail[:, 0:6].reshape(chunks, 2, 3, part).sum(2).reshape(chunks, own)
    loss = tail[:, 6:12].reshape(chunks, 2, 3, part).sum((0, 2)).reshape(own)
    sums_d = tail[:, 12:15].sum(1)
    new_mean = jnp.sum(sums_t, axis=0) / all_tokens
    mean_d = jnp.sum(sums_d, axis=0) / all_tokens
    off_t = sums_t / rows - new_mean
    off_d = sums_d / rows - mean_d
    between = lax.dot_general(
        off_t, off_d, (((0,), (0,)), ((), ())), precision=lax.Precision.HIGHEST, preferred_element_type=F32
    )
    new_cov = (within_sum + between * rows) / all_tokens
    return (new_cov, new_mean, grad_head, loss / image_count)


def solution(mesh):
    z, y, x = 8, 4, 4
    if mesh.devices.size != 512:
        z, y, x = 2, mesh.shape["dp"] // 2, mesh.shape["tensor"] // 4
    inner = Mesh(mesh.devices.reshape(z, y, x, 2, 2), DP + TN)
    return jax.shard_map(
        body,
        mesh=inner,
        in_specs=(
            P(DP, TN),
            P(TN, DP),
            P(),
            P(),
            P(None, TN),
            P(TN),
            P(),
            P(DP, None),
            P(None, TN),
            P(),
        ),
        out_specs=(P(TN, DP), P(TN), P(None, TN), P(TN)),
        check_vma=False,
    )
```

```python
import jax
import jax.numpy as jnp
from jax import lax
from jax.experimental import pallas as pl
from jax.experimental.pallas import tpu as pltpu
from jax.sharding import Mesh
from jax.sharding import PartitionSpec as P

DP = ("z", "yh")
TN = ("x", "yl", "c")
IMAGE_SHARE = 128
BF = jnp.bfloat16
F32 = jnp.float32


def hold(value):
    return lax.reduce_precision(value, 8, 7)


def split3(value):
    high = hold(value)
    rest = value - high
    mid = hold(rest)
    return high, mid, rest - mid


def broadcast_gather(block, axes):
    count = lax.axis_size(axes)
    return lax.all_to_all(jnp.broadcast_to(block[None], (count,) + block.shape), axes, 0, 0, tiled=True)


def shift(block, axis, step):
    count = lax.axis_size(axis)
    return lax.ppermute(block, axis, [(i, (i + step) % count) for i in range(count)])


def tensor_gather(block):
    mine = broadcast_gather(block, TN[:2])
    return mine, lax.ppermute(mine, "c", [(0, 1), (1, 0)])


def tensor_gather_twice(block):
    other = lax.ppermute(block, "c", [(0, 1), (1, 0)])
    return broadcast_gather(block, TN[:2]), broadcast_gather(other, TN[:2])


def parity_sign(value):
    count = jnp.zeros_like(value)
    for place in range(16):
        count = count + (value >> place & 1)
    return 1 - 2 * (count % 2)


def layer_norm(values):
    centred = values - jnp.mean(values, axis=-1, keepdims=True)
    spread = jnp.mean(centred * centred, axis=-1, keepdims=True)
    return centred * lax.rsqrt(spread + 1e-06)


def fetch(copies):
    for copy in copies:
        copy.start()
    return copies


def project_kernel(pos_ref, mine_hbm, other_hbm, w_hbm, out_ref, stat_ref, x_ref, w_ref, x_sem, w_sem):
    count, own = x_ref.shape[0], x_ref.shape[2]
    core = lax.rem(pos_ref[0], 2)
    order = [(mine_hbm, q, 2 * q + core) for q in range(count // 2)]
    order += [(other_hbm, q, 2 * q + 1 - core) for q in range(count // 2)]
    x_copies, w_copies = [], []
    for j, (source, q, b) in enumerate(order):
        x_copies += fetch([pltpu.make_async_copy(source.at[q], x_ref.at[j], x_sem.at[j])])
        w_copies += fetch([pltpu.make_async_copy(w_hbm.at[b], w_ref.at[j], w_sem.at[j])])
    total = jnp.zeros(out_ref.shape, F32)
    for j in range(count):
        x_copies[j].wait()
        w_copies[j].wait()
        total += jnp.dot(x_ref[j], w_ref[j], preferred_element_type=F32)
    mean = jnp.sum(total, axis=1, keepdims=True) * (1.0 / own)
    centred = total - mean
    out_ref[...] = centred.astype(BF)
    spread = jnp.sum(centred * centred, axis=1, keepdims=True)
    lane = lax.broadcasted_iota(jnp.int32, stat_ref.shape, 1)
    stat_ref[...] = jnp.where(lane == 0, mean, spread)


def feature_kernel(
    pos_ref, mine_ref, other_ref, adj_ref, rstd_ref, gain_ref, prev_ref, rot_ref, sign_ref,
    f_ref, basis_ref, sums_ref,
):
    blocks, rows, own = f_ref.shape
    core = lax.rem(pos_ref[0], 2)
    rstd = rstd_ref[...]
    total = jnp.zeros((rows, own), F32)
    for j in range(blocks):
        source, q, side = (mine_ref, j, core) if j < blocks // 2 else (other_ref, j - blocks // 2, 1 - core)
        b = 2 * q + side
        value = (source[q, :rows, :].astype(F32) + adj_ref[:, j : j + 1]) * rstd * gain_ref[b]
        feature = value.astype(BF)
        f_ref[b] = feature
        feature = feature.astype(F32)
        sums_ref[b] = jnp.sum(feature, axis=0, keepdims=True)
        shifted = (feature - prev_ref[b]).astype(BF)
        turn = rot_ref[pl.ds(pl.multiple_of(b * own, own), own), :]
        total += jnp.dot(shifted, turn, preferred_element_type=F32)
    basis_ref[...] = total.astype(BF) * sign_ref[...]


def moment_kernel(pos_ref, f_ref, sums_ref, out_ref):
    blocks, rows, own = f_ref.shape
    part = out_ref.shape[2]
    own_t = f_ref[pos_ref[0]].astype(F32).T
    own_col = jnp.sum(own_t, axis=1, keepdims=True)
    own_t = own_t.astype(BF)
    for b in range(blocks):
        block = jnp.dot(own_t, f_ref[b], preferred_element_type=F32) - own_col * (sums_ref[b] * (1.0 / rows))
        block = block.astype(BF)
        for h in range(2):
            out_ref[2 * b + h] = block[:, h * part : (h + 1) * part]


def hadamard_kernel(scale_ref, basis_ref, table_ref, out_ref):
    blocks, few, own = basis_ref.shape
    flat = basis_ref[...].reshape(blocks * few, own)
    mixed = jnp.dot(flat, table_ref[...], preferred_element_type=F32) * scale_ref[0]
    parts = [mixed[b * few : (b + 1) * few] for b in range(blocks)]
    step = 1
    while step < blocks:
        parts = [
            parts[b - step] - parts[b] if b & step else parts[b] + parts[b + step] for b in range(blocks)
        ]
        step *= 2
    for b in range(blocks):
        out_ref[b] = parts[b].astype(BF)


def grad_kernel(pos_ref, target_ref, pred_ref, w_ref, normed_ref, sums_ref, out_ref):
    chunks, _, part = out_ref.shape
    depth = normed_ref.shape[1] // chunks
    residual = pred_ref[...] - target_ref[...].astype(F32)
    weighted = residual * w_ref[...]
    loss = jnp.sum(weighted * residual, axis=0, keepdims=True)
    grad = lax.dot_general(
        normed_ref[...], weighted.astype(BF), (((0,), (0,)), ((), ())), preferred_element_type=F32
    ).astype(BF)
    row = lax.broadcasted_iota(jnp.int32, (16, part), 0)

    def parts(value):
        high = value.astype(BF).astype(F32)
        rest = value - high
        mid = rest.astype(BF).astype(F32)
        return [high, mid, rest - mid]

    own_row = sums_ref[pos_ref[0]]
    fixed = []
    for h in range(2):
        fixed += parts(own_row[:, h * part : (h + 1) * part])
    for h in range(2):
        fixed += parts(loss[:, h * part : (h + 1) * part])
    for d in range(chunks):
        for h in range(2):
            out_ref[d, h * depth : (h + 1) * depth, :] = grad[
                d * depth : (d + 1) * depth, h * part : (h + 1) * part
            ]
        tile = jnp.zeros((16, part), F32)
        here = sums_ref[d // 2][:, (d % 2) * part : (d % 2 + 1) * part]
        for i, piece in enumerate(fixed + parts(here)):
            tile = jnp.where(row == i, piece, tile)
        out_ref[d, 2 * depth :, :] = tile.astype(BF)


def place_kernel(in_ref, out_ref):
    chunks, tall, part = in_ref.shape
    depth = tall // 2
    for d in range(chunks):
        for h in range(2):
            out_ref[d * depth : (d + 1) * depth, h * part : (h + 1) * part] = in_ref[
                d, h * depth : (h + 1) * depth, :
            ].astype(F32)


def body(
    teacher_in,
    out_proj,
    final_gain,
    mean_prev,
    rotation,
    signs,
    prev_scale,
    student_in,
    head_weight,
    image_ids,
):
    rows, own = teacher_in.shape
    part = out_proj.shape[1]
    width = final_gain.shape[0]
    blocks = width // own
    chunks = width // part
    depth = student_in.shape[1] // chunks
    all_tokens = image_ids.shape[0]
    image_count = all_tokens // IMAGE_SHARE
    dpos = lax.axis_index(DP)
    tpos = lax.axis_index(TN)

    side = dpos % 2
    halves = out_proj.reshape(2, part, part)
    got = []
    for k in range(2):
        send = lax.dynamic_index_in_dim(halves, (side + k) % 2, 0, keepdims=False)
        route = []
        for d in range(chunks):
            for t in range(blocks):
                route.append((d * blocks + t, (2 * t + (d % 2 ^ k)) * blocks + d // 2))
        got.append(lax.ppermute(send, DP + TN, route))
    strip = jnp.where(
        side == 0, jnp.concatenate(got, axis=1), jnp.concatenate(got[::-1], axis=1)
    )
    near = broadcast_gather(strip, "yh")
    proj = lax.all_gather(near.reshape(-1, own), "z", axis=0, tiled=True)
    teacher, _ = lax.optimization_barrier((teacher_in, near))
    positive = prev_scale[0] > 0.0
    teacher = lax.cond(positive, tensor_gather, tensor_gather_twice, teacher)

    normed = layer_norm(student_in.astype(F32)).astype(BF)
    predicted = jnp.dot(normed, head_weight, preferred_element_type=F32)
    image_nums = jnp.arange(image_count, dtype=jnp.int32)
    counts = jnp.sum((image_ids[None, :] == image_nums[:, None]).astype(F32), axis=1)
    own_ids = lax.dynamic_slice_in_dim(image_ids, dpos * rows, rows, 0)
    token_counts = jnp.sum(
        jnp.where(own_ids[:, None] == image_nums[None, :], counts[None, :], 0.0), axis=1, keepdims=True
    )
    token_weight = 1.0 / token_counts

    smem, vmem = pl.BlockSpec(memory_space=pltpu.SMEM), pl.BlockSpec(memory_space=pltpu.VMEM)
    anywhere = pl.BlockSpec(memory_space=pl.ANY)
    position = tpos.reshape(1)
    raw, stat = pl.pallas_call(
        project_kernel,
        out_shape=(jax.ShapeDtypeStruct((rows, own), BF), jax.ShapeDtypeStruct((rows, 2), F32)),
        in_specs=[smem] + [anywhere] * 3,
        out_specs=(vmem, vmem),
        scratch_shapes=[
            pltpu.VMEM((blocks, rows, own), BF),
            pltpu.VMEM((blocks, own, own), BF),
            pltpu.SemaphoreType.DMA((blocks,)),
            pltpu.SemaphoreType.DMA((blocks,)),
        ],
        compiler_params=pltpu.CompilerParams(vmem_limit_bytes=52 << 20),
        cost_estimate=pl.CostEstimate(flops=2 * rows * width * own, bytes_accessed=8 << 20, transcendentals=0),
    )(position, *teacher, proj.reshape(blocks, own, own))
    pieces = jnp.stack(split3(stat.T)).reshape(6 * rows // own, own).astype(BF)
    spare = -pieces.shape[0] % 16
    packed = jnp.concatenate([raw, pieces, jnp.zeros((spare, own), BF)])
    mine, other = tensor_gather(packed)
    first = tpos % 2 == 0

    def unpack(block):
        tail = block[:, rows : rows + pieces.shape[0], :].astype(F32)
        return tail.reshape(blocks // 2, 3, 2, rows).sum(1)

    stat_mine, stat_other = unpack(mine), unpack(other)
    stats = jnp.stack(
        [jnp.where(first, stat_mine, stat_other), jnp.where(first, stat_other, stat_mine)], axis=1
    ).reshape(blocks, 2, rows)
    mean = jnp.mean(stats[:, 0], axis=0)
    adjust = stats[:, 0] - mean
    variance = (jnp.sum(stats[:, 1], axis=0) + own * jnp.sum(adjust * adjust, axis=0)) / width
    rstd = lax.rsqrt(variance + 1e-06)
    adjust = jnp.concatenate([stat_mine[:, 0], stat_other[:, 0]]) - mean
    scale = 1.0 / (jnp.sqrt(F32(width)) * prev_scale)
    index_row = lax.broadcasted_iota(jnp.int32, (own, own), 0)
    index_col = lax.broadcasted_iota(jnp.int32, (own, own), 1)
    table = parity_sign(index_row & index_col).astype(BF)

    features, basis, sums = pl.pallas_call(
        feature_kernel,
        out_shape=(
            jax.ShapeDtypeStruct((blocks, rows, own), BF),
            jax.ShapeDtypeStruct((rows, own), BF),
            jax.ShapeDtypeStruct((blocks, 1, own), F32),
        ),
        in_specs=[smem] + [vmem] * 8,
        out_specs=(vmem,) * 3,
        compiler_params=pltpu.CompilerParams(vmem_limit_bytes=16 << 20),
        cost_estimate=pl.CostEstimate(flops=2 * rows * width * own, bytes_accessed=12 << 20, transcendentals=0),
    )(
        position,
        mine,
        other,
        adjust.T,
        rstd[:, None],
        final_gain.reshape(blocks, 1, own),
        mean_prev.reshape(blocks, 1, own),
        rotation,
        (2 * signs - 1).astype(BF)[None, :],
    )
    lines = lax.all_to_all(basis.reshape(blocks, rows // blocks, own), TN, 0, 0, tiled=True)
    moment = pl.pallas_call(
        moment_kernel,
        out_shape=jax.ShapeDtypeStruct((chunks, own, part), BF),
        in_specs=[smem, vmem, vmem],
        out_specs=vmem,
        compiler_params=pltpu.CompilerParams(vmem_limit_bytes=12 << 20),
        cost_estimate=pl.CostEstimate(flops=2 * rows * width * own, bytes_accessed=6 << 20, transcendentals=0),
    )(position, features, sums)
    within = lax.psum_scatter(moment, "z", scatter_dimension=0, tiled=True)

    lines = pl.pallas_call(
        hadamard_kernel,
        out_shape=jax.ShapeDtypeStruct(lines.shape, BF),
        in_specs=[smem, vmem, vmem],
        out_specs=vmem,
        compiler_params=pltpu.CompilerParams(vmem_limit_bytes=12 << 20),
    )(scale, lines, table)
    target = lax.all_to_all(lines, TN, 0, 0, tiled=True).reshape(rows, own)

    sent = pl.pallas_call(
        grad_kernel,
        out_shape=jax.ShapeDtypeStruct((chunks, 2 * depth + 16, part), BF),
        in_specs=[smem] + [vmem] * 5,
        out_specs=vmem,
        compiler_params=pltpu.CompilerParams(vmem_limit_bytes=12 << 20),
    )(position, target, predicted, token_weight, normed, sums)
    taken = lax.all_to_all(sent, DP, 0, 0, tiled=True)

    grad_own = jnp.sum(taken[:, : 2 * depth, :].astype(F32), axis=0).astype(BF)
    within = lax.psum_scatter(within, "yh", scatter_dimension=0, tiled=True)
    grads = lax.cond(
        positive,
        lambda block: broadcast_gather(block, DP),
        lambda block: lax.all_gather(block, DP, axis=0, tiled=False),
        grad_own,
    )
    grad_head = pl.pallas_call(
        place_kernel,
        out_shape=jax.ShapeDtypeStruct((chunks * depth, own), F32),
        in_specs=[vmem],
        out_specs=vmem,
    )(grads)

    tail = taken[:, 2 * depth :, :].astype(F32)
    sums_t = tail[:, 0:6].reshape(chunks, 2, 3, part).sum(2).reshape(chunks, own)
    loss = tail[:, 6:12].reshape(chunks, 2, 3, part).sum((0, 2)).reshape(own)
    sums_d = tail[:, 12:15].sum(1)
    new_mean = jnp.sum(sums_t, axis=0) / all_tokens
    mean_d = jnp.sum(sums_d, axis=0) / all_tokens
    off_t = sums_t / rows - new_mean
    off_d = sums_d / rows - mean_d
    between = lax.dot_general(
        off_t, off_d, (((0,), (0,)), ((), ())), precision=lax.Precision.HIGHEST, preferred_element_type=F32
    )
    new_cov = (within.reshape(own, part).astype(F32) + between * rows) / all_tokens
    return (new_cov, new_mean, grad_head, loss / image_count)


def solution(mesh):
    z, y, x = 8, 4, 4
    if mesh.devices.size != 512:
        z, y, x = 2, mesh.shape["dp"] // 2, mesh.shape["tensor"] // 4
    inner = Mesh(mesh.devices.reshape(z, y, x, 2, 2), DP + TN)
    return jax.shard_map(
        body,
        mesh=inner,
        in_specs=(
            P(DP, TN),
            P(TN, DP),
            P(),
            P(),
            P(None, TN),
            P(TN),
            P(),
            P(DP, None),
            P(None, TN),
            P(),
        ),
        out_specs=(P(TN, DP), P(TN), P(None, TN), P(TN)),
        check_vma=False,
    )
```

```python
import jax
import jax.numpy as jnp
from jax import lax
from jax.experimental import pallas as pl
from jax.experimental.pallas import tpu as pltpu
from jax.sharding import Mesh
from jax.sharding import PartitionSpec as P

DP = ("z", "yh")
TN = ("x", "yl", "c")
IMAGE_SHARE = 128
BF = jnp.bfloat16
F32 = jnp.float32


def hold(value):
    return lax.reduce_precision(value, 8, 7)


def split3(value):
    high = hold(value)
    rest = value - high
    mid = hold(rest)
    return high, mid, rest - mid


def broadcast_gather(block, axes):
    count = lax.axis_size(axes)
    return lax.all_to_all(jnp.broadcast_to(block[None], (count,) + block.shape), axes, 0, 0, tiled=True)


def shift(block, axis, step):
    count = lax.axis_size(axis)
    return lax.ppermute(block, axis, [(i, (i + step) % count) for i in range(count)])


def tensor_gather(block):
    mine = broadcast_gather(block, TN[:2])
    return mine, lax.ppermute(mine, "c", [(0, 1), (1, 0)])


def tensor_gather_twice(block):
    other = lax.ppermute(block, "c", [(0, 1), (1, 0)])
    return broadcast_gather(block, TN[:2]), broadcast_gather(other, TN[:2])


def parity_sign(value):
    count = jnp.zeros_like(value)
    for place in range(16):
        count = count + (value >> place & 1)
    return 1 - 2 * (count % 2)


def layer_norm(values):
    centred = values - jnp.mean(values, axis=-1, keepdims=True)
    spread = jnp.mean(centred * centred, axis=-1, keepdims=True)
    return centred * lax.rsqrt(spread + 1e-06)


def fetch(copies):
    for copy in copies:
        copy.start()
    return copies


def project_kernel(pos_ref, mine_hbm, other_hbm, w_hbm, out_ref, stat_ref, x_ref, w_ref, x_sem, w_sem):
    count, own = x_ref.shape[0], x_ref.shape[2]
    core = lax.rem(pos_ref[0], 2)
    order = [(mine_hbm, q, 2 * q + core) for q in range(count // 2)]
    order += [(other_hbm, q, 2 * q + 1 - core) for q in range(count // 2)]
    x_copies, w_copies = [], []
    for j, (source, q, b) in enumerate(order):
        x_copies += fetch([pltpu.make_async_copy(source.at[q], x_ref.at[j], x_sem.at[j])])
        w_copies += fetch([pltpu.make_async_copy(w_hbm.at[b], w_ref.at[j], w_sem.at[j])])
    total = jnp.zeros(out_ref.shape, F32)
    for j in range(count):
        x_copies[j].wait()
        w_copies[j].wait()
        total += jnp.dot(x_ref[j], w_ref[j], preferred_element_type=F32)
    mean = jnp.sum(total, axis=1, keepdims=True) * (1.0 / own)
    centred = total - mean
    out_ref[...] = centred.astype(BF)
    spread = jnp.sum(centred * centred, axis=1, keepdims=True)
    lane = lax.broadcasted_iota(jnp.int32, stat_ref.shape, 1)
    stat_ref[...] = jnp.where(lane == 0, mean, spread)


def feature_kernel(
    pos_ref, mine_ref, other_ref, adj_ref, rstd_ref, gain_ref, prev_ref, rot_ref, sign_ref,
    f_ref, basis_ref, sums_ref,
):
    blocks, rows, own = f_ref.shape
    core = lax.rem(pos_ref[0], 2)
    rstd = rstd_ref[...]
    total = jnp.zeros((rows, own), F32)
    for j in range(blocks):
        source, q, side = (mine_ref, j, core) if j < blocks // 2 else (other_ref, j - blocks // 2, 1 - core)
        b = 2 * q + side
        value = (source[q, :rows, :].astype(F32) + adj_ref[:, j : j + 1]) * rstd * gain_ref[b]
        feature = value.astype(BF)
        f_ref[b] = feature
        feature = feature.astype(F32)
        sums_ref[b] = jnp.sum(feature, axis=0, keepdims=True)
        shifted = (feature - prev_ref[b]).astype(BF)
        turn = rot_ref[pl.ds(pl.multiple_of(b * own, own), own), :]
        total += jnp.dot(shifted, turn, preferred_element_type=F32)
    basis_ref[...] = total.astype(BF) * sign_ref[...]


def moment_kernel(pos_ref, f_ref, sums_ref, out_ref):
    blocks, rows, own = f_ref.shape
    part = out_ref.shape[2]
    own_t = f_ref[pos_ref[0]].astype(F32).T
    own_col = jnp.sum(own_t, axis=1, keepdims=True)
    own_t = own_t.astype(BF)
    for b in range(blocks):
        block = jnp.dot(own_t, f_ref[b], preferred_element_type=F32) - own_col * (sums_ref[b] * (1.0 / rows))
        block = block.astype(BF)
        for h in range(2):
            out_ref[2 * b + h] = block[:, h * part : (h + 1) * part]


def hadamard_kernel(scale_ref, basis_ref, table_ref, out_ref):
    blocks, few, own = basis_ref.shape
    flat = basis_ref[...].reshape(blocks * few, own)
    mixed = jnp.dot(flat, table_ref[...], preferred_element_type=F32) * scale_ref[0]
    parts = [mixed[b * few : (b + 1) * few] for b in range(blocks)]
    step = 1
    while step < blocks:
        parts = [
            parts[b - step] - parts[b] if b & step else parts[b] + parts[b + step] for b in range(blocks)
        ]
        step *= 2
    for b in range(blocks):
        out_ref[b] = parts[b].astype(BF)


def grad_kernel(pos_ref, target_ref, pred_ref, w_ref, normed_ref, sums_ref, out_ref):
    chunks, _, part = out_ref.shape
    depth = normed_ref.shape[1] // chunks
    residual = pred_ref[...] - target_ref[...].astype(F32)
    weighted = residual * w_ref[...]
    loss = jnp.sum(weighted * residual, axis=0, keepdims=True)
    grad = lax.dot_general(
        normed_ref[...], weighted.astype(BF), (((0,), (0,)), ((), ())), preferred_element_type=F32
    ).astype(BF)
    row = lax.broadcasted_iota(jnp.int32, (16, part), 0)

    def parts(value):
        high = value.astype(BF).astype(F32)
        rest = value - high
        mid = rest.astype(BF).astype(F32)
        return [high, mid, rest - mid]

    own_row = sums_ref[pos_ref[0]]
    fixed = []
    for h in range(2):
        fixed += parts(own_row[:, h * part : (h + 1) * part])
    for h in range(2):
        fixed += parts(loss[:, h * part : (h + 1) * part])
    for d in range(chunks):
        for h in range(2):
            out_ref[d, h * depth : (h + 1) * depth, :] = grad[
                d * depth : (d + 1) * depth, h * part : (h + 1) * part
            ]
        tile = jnp.zeros((16, part), F32)
        here = sums_ref[d // 2][:, (d % 2) * part : (d % 2 + 1) * part]
        for i, piece in enumerate(fixed + parts(here)):
            tile = jnp.where(row == i, piece, tile)
        out_ref[d, 2 * depth :, :] = tile.astype(BF)


def place_kernel(in_ref, out_ref):
    chunks, tall, part = in_ref.shape
    depth = tall // 2
    for d in range(chunks):
        for h in range(2):
            out_ref[d * depth : (d + 1) * depth, h * part : (h + 1) * part] = in_ref[
                d, h * depth : (h + 1) * depth, :
            ].astype(F32)


def body(
    teacher_in,
    out_proj,
    final_gain,
    mean_prev,
    rotation,
    signs,
    prev_scale,
    student_in,
    head_weight,
    image_ids,
):
    rows, own = teacher_in.shape
    part = out_proj.shape[1]
    width = final_gain.shape[0]
    blocks = width // own
    chunks = width // part
    depth = student_in.shape[1] // chunks
    all_tokens = image_ids.shape[0]
    image_count = all_tokens // IMAGE_SHARE
    dpos = lax.axis_index(DP)
    tpos = lax.axis_index(TN)

    side = dpos % 2
    halves = out_proj.reshape(2, part, part)
    got = []
    for k in range(2):
        send = lax.dynamic_index_in_dim(halves, (side + k) % 2, 0, keepdims=False)
        route = []
        for d in range(chunks):
            for t in range(blocks):
                route.append((d * blocks + t, (2 * t + (d % 2 ^ k)) * blocks + d // 2))
        got.append(lax.ppermute(send, DP + TN, route))
    strip = jnp.where(
        side == 0, jnp.concatenate(got, axis=1), jnp.concatenate(got[::-1], axis=1)
    )
    near = broadcast_gather(strip, "yh")
    proj = lax.all_gather(near.reshape(-1, own), "z", axis=0, tiled=True)
    teacher, _ = lax.optimization_barrier((teacher_in, near))
    positive = prev_scale[0] > 0.0
    teacher = lax.cond(positive, tensor_gather, tensor_gather_twice, teacher)
    teacher, image_ids = lax.optimization_barrier((teacher, image_ids))

    normed = layer_norm(student_in.astype(F32)).astype(BF)
    predicted = jnp.dot(normed, head_weight, preferred_element_type=F32)
    image_nums = jnp.arange(image_count, dtype=jnp.int32)
    counts = jnp.sum((image_ids[None, :] == image_nums[:, None]).astype(F32), axis=1)
    own_ids = lax.dynamic_slice_in_dim(image_ids, dpos * rows, rows, 0)
    token_counts = jnp.sum(
        jnp.where(own_ids[:, None] == image_nums[None, :], counts[None, :], 0.0), axis=1, keepdims=True
    )
    token_weight = 1.0 / token_counts

    smem, vmem = pl.BlockSpec(memory_space=pltpu.SMEM), pl.BlockSpec(memory_space=pltpu.VMEM)
    anywhere = pl.BlockSpec(memory_space=pl.ANY)
    position = tpos.reshape(1)
    proj, token_weight = lax.optimization_barrier((proj, token_weight))
    raw, stat = pl.pallas_call(
        project_kernel,
        out_shape=(jax.ShapeDtypeStruct((rows, own), BF), jax.ShapeDtypeStruct((rows, 2), F32)),
        in_specs=[smem] + [anywhere] * 3,
        out_specs=(vmem, vmem),
        scratch_shapes=[
            pltpu.VMEM((blocks, rows, own), BF),
            pltpu.VMEM((blocks, own, own), BF),
            pltpu.SemaphoreType.DMA((blocks,)),
            pltpu.SemaphoreType.DMA((blocks,)),
        ],
        compiler_params=pltpu.CompilerParams(vmem_limit_bytes=52 << 20),
        cost_estimate=pl.CostEstimate(flops=2 * rows * width * own, bytes_accessed=8 << 20, transcendentals=0),
    )(position, *teacher, proj.reshape(blocks, own, own))
    pieces = jnp.stack(split3(stat.T)).reshape(6 * rows // own, own).astype(BF)
    spare = -pieces.shape[0] % 16
    packed = jnp.concatenate([raw, pieces, jnp.zeros((spare, own), BF)])
    mine, other = tensor_gather(packed)
    first = tpos % 2 == 0

    def unpack(block):
        tail = block[:, rows : rows + pieces.shape[0], :].astype(F32)
        return tail.reshape(blocks // 2, 3, 2, rows).sum(1)

    stat_mine, stat_other = unpack(mine), unpack(other)
    stats = jnp.stack(
        [jnp.where(first, stat_mine, stat_other), jnp.where(first, stat_other, stat_mine)], axis=1
    ).reshape(blocks, 2, rows)
    mean = jnp.mean(stats[:, 0], axis=0)
    adjust = stats[:, 0] - mean
    variance = (jnp.sum(stats[:, 1], axis=0) + own * jnp.sum(adjust * adjust, axis=0)) / width
    rstd = lax.rsqrt(variance + 1e-06)
    adjust = jnp.concatenate([stat_mine[:, 0], stat_other[:, 0]]) - mean
    scale = 1.0 / (jnp.sqrt(F32(width)) * prev_scale)
    index_row = lax.broadcasted_iota(jnp.int32, (own, own), 0)
    index_col = lax.broadcasted_iota(jnp.int32, (own, own), 1)
    table = parity_sign(index_row & index_col).astype(BF)

    features, basis, sums = pl.pallas_call(
        feature_kernel,
        out_shape=(
            jax.ShapeDtypeStruct((blocks, rows, own), BF),
            jax.ShapeDtypeStruct((rows, own), BF),
            jax.ShapeDtypeStruct((blocks, 1, own), F32),
        ),
        in_specs=[smem] + [vmem] * 8,
        out_specs=(vmem,) * 3,
        compiler_params=pltpu.CompilerParams(vmem_limit_bytes=16 << 20),
        cost_estimate=pl.CostEstimate(flops=2 * rows * width * own, bytes_accessed=12 << 20, transcendentals=0),
    )(
        position,
        mine,
        other,
        adjust.T,
        rstd[:, None],
        final_gain.reshape(blocks, 1, own),
        mean_prev.reshape(blocks, 1, own),
        rotation,
        (2 * signs - 1).astype(BF)[None, :],
    )
    lines = lax.all_to_all(basis.reshape(blocks, rows // blocks, own), TN, 0, 0, tiled=True)
    moment = pl.pallas_call(
        moment_kernel,
        out_shape=jax.ShapeDtypeStruct((chunks, own, part), BF),
        in_specs=[smem, vmem, vmem],
        out_specs=vmem,
        compiler_params=pltpu.CompilerParams(vmem_limit_bytes=12 << 20),
        cost_estimate=pl.CostEstimate(flops=2 * rows * width * own, bytes_accessed=6 << 20, transcendentals=0),
    )(position, features, sums)
    within = lax.psum_scatter(moment, "z", scatter_dimension=0, tiled=True)

    lines = pl.pallas_call(
        hadamard_kernel,
        out_shape=jax.ShapeDtypeStruct(lines.shape, BF),
        in_specs=[smem, vmem, vmem],
        out_specs=vmem,
        compiler_params=pltpu.CompilerParams(vmem_limit_bytes=12 << 20),
    )(scale, lines, table)
    target = lax.all_to_all(lines, TN, 0, 0, tiled=True).reshape(rows, own)

    sent = pl.pallas_call(
        grad_kernel,
        out_shape=jax.ShapeDtypeStruct((chunks, 2 * depth + 16, part), BF),
        in_specs=[smem] + [vmem] * 5,
        out_specs=vmem,
        compiler_params=pltpu.CompilerParams(vmem_limit_bytes=12 << 20),
    )(position, target, predicted, token_weight, normed, sums)
    taken = lax.all_to_all(sent, DP, 0, 0, tiled=True)

    grad_own = jnp.sum(taken[:, : 2 * depth, :].astype(F32), axis=0).astype(BF)
    within = lax.psum_scatter(within.astype(F32), "yh", scatter_dimension=0, tiled=True)
    grads = lax.cond(
        positive,
        lambda block: broadcast_gather(block, DP),
        lambda block: lax.all_gather(block, DP, axis=0, tiled=False),
        grad_own,
    )
    grad_head = pl.pallas_call(
        place_kernel,
        out_shape=jax.ShapeDtypeStruct((chunks * depth, own), F32),
        in_specs=[vmem],
        out_specs=vmem,
    )(grads)

    tail = taken[:, 2 * depth :, :].astype(F32)
    sums_t = tail[:, 0:6].reshape(chunks, 2, 3, part).sum(2).reshape(chunks, own)
    loss = tail[:, 6:12].reshape(chunks, 2, 3, part).sum((0, 2)).reshape(own)
    sums_d = tail[:, 12:15].sum(1)
    new_mean = jnp.sum(sums_t, axis=0) / all_tokens
    mean_d = jnp.sum(sums_d, axis=0) / all_tokens
    off_t = sums_t / rows - new_mean
    off_d = sums_d / rows - mean_d
    between = lax.dot_general(
        off_t, off_d, (((0,), (0,)), ((), ())), precision=lax.Precision.HIGHEST, preferred_element_type=F32
    )
    new_cov = (within.reshape(own, part) + between * rows) / all_tokens
    return (new_cov, new_mean, grad_head, loss / image_count)


def solution(mesh):
    z, y, x = 8, 4, 4
    if mesh.devices.size != 512:
        z, y, x = 2, mesh.shape["dp"] // 2, mesh.shape["tensor"] // 4
    inner = Mesh(mesh.devices.reshape(z, y, x, 2, 2), DP + TN)
    return jax.shard_map(
        body,
        mesh=inner,
        in_specs=(
            P(DP, TN),
            P(TN, DP),
            P(),
            P(),
            P(None, TN),
            P(TN),
            P(),
            P(DP, None),
            P(None, TN),
            P(),
        ),
        out_specs=(P(TN, DP), P(TN), P(None, TN), P(TN)),
        check_vma=False,
    )
```

```python
import jax
import jax.numpy as jnp
from jax import lax
from jax.experimental import pallas as pl
from jax.experimental.pallas import tpu as pltpu
from jax.sharding import Mesh
from jax.sharding import PartitionSpec as P

DP = ("z", "yh")
TN = ("x", "yl", "c")
IMAGE_SHARE = 128
BF = jnp.bfloat16
F32 = jnp.float32


def hold(value):
    return lax.reduce_precision(value, 8, 7)


def split3(value):
    high = hold(value)
    rest = value - high
    mid = hold(rest)
    return high, mid, rest - mid


def broadcast_gather(block, axes):
    count = lax.axis_size(axes)
    return lax.all_to_all(jnp.broadcast_to(block[None], (count,) + block.shape), axes, 0, 0, tiled=True)


def shift(block, axis, step):
    count = lax.axis_size(axis)
    return lax.ppermute(block, axis, [(i, (i + step) % count) for i in range(count)])


def tensor_gather(block):
    mine = broadcast_gather(block, TN[:2])
    return mine, lax.ppermute(mine, "c", [(0, 1), (1, 0)])


def tensor_gather_twice(block):
    other = lax.ppermute(block, "c", [(0, 1), (1, 0)])
    return broadcast_gather(block, TN[:2]), broadcast_gather(other, TN[:2])


def parity_sign(value):
    count = jnp.zeros_like(value)
    for place in range(16):
        count = count + (value >> place & 1)
    return 1 - 2 * (count % 2)


def layer_norm(values):
    centred = values - jnp.mean(values, axis=-1, keepdims=True)
    spread = jnp.mean(centred * centred, axis=-1, keepdims=True)
    return centred * lax.rsqrt(spread + 1e-06)


def fetch(copies):
    for copy in copies:
        copy.start()
    return copies


def project_kernel(pos_ref, mine_hbm, other_hbm, w_hbm, out_ref, stat_ref, x_ref, w_ref, x_sem, w_sem):
    count, own = x_ref.shape[0], x_ref.shape[2]
    core = lax.rem(pos_ref[0], 2)
    order = [(mine_hbm, q, 2 * q + core) for q in range(count // 2)]
    order += [(other_hbm, q, 2 * q + 1 - core) for q in range(count // 2)]
    x_copies, w_copies = [], []
    for j, (source, q, b) in enumerate(order):
        x_copies += fetch([pltpu.make_async_copy(source.at[q], x_ref.at[j], x_sem.at[j])])
        w_copies += fetch([pltpu.make_async_copy(w_hbm.at[b], w_ref.at[j], w_sem.at[j])])
    total = jnp.zeros(out_ref.shape, F32)
    for j in range(count):
        x_copies[j].wait()
        w_copies[j].wait()
        total += jnp.dot(x_ref[j], w_ref[j], preferred_element_type=F32)
    mean = jnp.sum(total, axis=1, keepdims=True) * (1.0 / own)
    centred = total - mean
    out_ref[...] = centred.astype(BF)
    spread = jnp.sum(centred * centred, axis=1, keepdims=True)
    lane = lax.broadcasted_iota(jnp.int32, stat_ref.shape, 1)
    stat_ref[...] = jnp.where(lane == 0, mean, spread)


def feature_kernel(
    pos_ref, mine_ref, other_ref, adj_ref, rstd_ref, gain_ref, prev_ref, rot_ref, sign_ref,
    f_ref, basis_ref, sums_ref,
):
    blocks, rows, own = f_ref.shape
    core = lax.rem(pos_ref[0], 2)
    rstd = rstd_ref[...]
    total = jnp.zeros((rows, own), F32)
    offset = jnp.zeros((16, own), F32)
    for j in range(blocks):
        source, q, side = (mine_ref, j, core) if j < blocks // 2 else (other_ref, j - blocks // 2, 1 - core)
        b = 2 * q + side
        value = (source[q, :rows, :].astype(F32) + adj_ref[:, j : j + 1]) * rstd * gain_ref[b]
        feature = value.astype(BF)
        f_ref[b] = feature
        sums_ref[b] = jnp.sum(feature.astype(F32), axis=0, keepdims=True)
        turn = rot_ref[pl.ds(pl.multiple_of(b * own, own), own), :]
        total += jnp.dot(feature, turn, preferred_element_type=F32)
        offset += jnp.dot(prev_ref[b], turn, preferred_element_type=F32)
    total -= jnp.sum(offset, axis=0, keepdims=True)
    basis_ref[...] = total.astype(BF) * sign_ref[...]


def moment_kernel(pos_ref, f_ref, sums_ref, out_ref):
    blocks, rows, own = f_ref.shape
    part = out_ref.shape[2]
    own_t = f_ref[pos_ref[0]].astype(F32).T
    own_col = jnp.sum(own_t, axis=1, keepdims=True)
    own_t = own_t.astype(BF)
    for b in range(blocks):
        block = jnp.dot(own_t, f_ref[b], preferred_element_type=F32) - own_col * (sums_ref[b] * (1.0 / rows))
        block = block.astype(BF)
        for h in range(2):
            out_ref[2 * b + h] = block[:, h * part : (h + 1) * part]


def hadamard_kernel(scale_ref, basis_ref, table_ref, out_ref):
    blocks, few, own = basis_ref.shape
    flat = basis_ref[...].reshape(blocks * few, own)
    mixed = jnp.dot(flat, table_ref[...], preferred_element_type=F32) * scale_ref[0]
    parts = [mixed[b * few : (b + 1) * few] for b in range(blocks)]
    step = 1
    while step < blocks:
        parts = [
            parts[b - step] - parts[b] if b & step else parts[b] + parts[b + step] for b in range(blocks)
        ]
        step *= 2
    for b in range(blocks):
        out_ref[b] = parts[b].astype(BF)


def grad_kernel(pos_ref, target_ref, pred_ref, w_ref, normed_ref, sums_ref, out_ref):
    chunks, _, part = out_ref.shape
    depth = normed_ref.shape[1] // chunks
    residual = pred_ref[...] - target_ref[...].astype(F32)
    weighted = residual * w_ref[...]
    loss = jnp.sum(weighted * residual, axis=0, keepdims=True)
    grad = lax.dot_general(
        normed_ref[...], weighted.astype(BF), (((0,), (0,)), ((), ())), preferred_element_type=F32
    ).astype(BF)
    row = lax.broadcasted_iota(jnp.int32, (16, part), 0)

    def parts(value):
        high = value.astype(BF).astype(F32)
        rest = value - high
        mid = rest.astype(BF).astype(F32)
        return [high, mid, rest - mid]

    own_row = sums_ref[pos_ref[0]]
    fixed = []
    for h in range(2):
        fixed += parts(own_row[:, h * part : (h + 1) * part])
    for h in range(2):
        fixed += parts(loss[:, h * part : (h + 1) * part])
    for d in range(chunks):
        for h in range(2):
            out_ref[d, h * depth : (h + 1) * depth, :] = grad[
                d * depth : (d + 1) * depth, h * part : (h + 1) * part
            ]
        tile = jnp.zeros((16, part), F32)
        here = sums_ref[d // 2][:, (d % 2) * part : (d % 2 + 1) * part]
        for i, piece in enumerate(fixed + parts(here)):
            tile = jnp.where(row == i, piece, tile)
        out_ref[d, 2 * depth :, :] = tile.astype(BF)


def place_kernel(in_ref, out_ref):
    chunks, tall, part = in_ref.shape
    depth = tall // 2
    for d in range(chunks):
        for h in range(2):
            out_ref[d * depth : (d + 1) * depth, h * part : (h + 1) * part] = in_ref[
                d, h * depth : (h + 1) * depth, :
            ].astype(F32)


def body(
    teacher_in,
    out_proj,
    final_gain,
    mean_prev,
    rotation,
    signs,
    prev_scale,
    student_in,
    head_weight,
    image_ids,
):
    rows, own = teacher_in.shape
    part = out_proj.shape[1]
    width = final_gain.shape[0]
    blocks = width // own
    chunks = width // part
    depth = student_in.shape[1] // chunks
    all_tokens = image_ids.shape[0]
    image_count = all_tokens // IMAGE_SHARE
    dpos = lax.axis_index(DP)
    tpos = lax.axis_index(TN)

    side = dpos % 2
    halves = out_proj.reshape(2, part, part)
    got = []
    for k in range(2):
        send = lax.dynamic_index_in_dim(halves, (side + k) % 2, 0, keepdims=False)
        route = []
        for d in range(chunks):
            for t in range(blocks):
                route.append((d * blocks + t, (2 * t + (d % 2 ^ k)) * blocks + d // 2))
        got.append(lax.ppermute(send, DP + TN, route))
    strip = jnp.where(
        side == 0, jnp.concatenate(got, axis=1), jnp.concatenate(got[::-1], axis=1)
    )
    near = broadcast_gather(strip, "yh")
    proj = lax.all_gather(near.reshape(-1, own), "z", axis=0, tiled=True)

    normed = layer_norm(student_in.astype(F32)).astype(BF)
    predicted = jnp.dot(normed, head_weight, preferred_element_type=F32)
    image_nums = jnp.arange(image_count, dtype=jnp.int32)
    counts = jnp.sum((image_ids[None, :] == image_nums[:, None]).astype(F32), axis=1)
    own_ids = lax.dynamic_slice_in_dim(image_ids, dpos * rows, rows, 0)
    token_counts = jnp.sum(
        jnp.where(own_ids[:, None] == image_nums[None, :], counts[None, :], 0.0), axis=1, keepdims=True
    )
    token_weight = 1.0 / token_counts

    smem, vmem = pl.BlockSpec(memory_space=pltpu.SMEM), pl.BlockSpec(memory_space=pltpu.VMEM)
    anywhere = pl.BlockSpec(memory_space=pl.ANY)
    position = tpos.reshape(1)
    teacher, _, token_weight = lax.optimization_barrier((teacher_in, near, token_weight))
    positive = prev_scale[0] > 0.0
    teacher = lax.cond(positive, tensor_gather, tensor_gather_twice, teacher)
    raw, stat = pl.pallas_call(
        project_kernel,
        out_shape=(jax.ShapeDtypeStruct((rows, own), BF), jax.ShapeDtypeStruct((rows, 2), F32)),
        in_specs=[smem] + [anywhere] * 3,
        out_specs=(vmem, vmem),
        scratch_shapes=[
            pltpu.VMEM((blocks, rows, own), BF),
            pltpu.VMEM((blocks, own, own), BF),
            pltpu.SemaphoreType.DMA((blocks,)),
            pltpu.SemaphoreType.DMA((blocks,)),
        ],
        compiler_params=pltpu.CompilerParams(vmem_limit_bytes=52 << 20),
        cost_estimate=pl.CostEstimate(flops=2 * rows * width * own, bytes_accessed=8 << 20, transcendentals=0),
    )(position, *teacher, proj.reshape(blocks, own, own))
    pieces = jnp.stack(split3(stat.T)).reshape(6 * rows // own, own).astype(BF)
    spare = -pieces.shape[0] % 16
    packed = jnp.concatenate([raw, pieces, jnp.zeros((spare, own), BF)])
    mine, other = tensor_gather(packed)
    first = tpos % 2 == 0

    def unpack(block):
        tail = block[:, rows : rows + pieces.shape[0], :].astype(F32)
        return tail.reshape(blocks // 2, 3, 2, rows).sum(1)

    stat_mine, stat_other = unpack(mine), unpack(other)
    stats = jnp.stack(
        [jnp.where(first, stat_mine, stat_other), jnp.where(first, stat_other, stat_mine)], axis=1
    ).reshape(blocks, 2, rows)
    mean = jnp.mean(stats[:, 0], axis=0)
    adjust = stats[:, 0] - mean
    variance = (jnp.sum(stats[:, 1], axis=0) + own * jnp.sum(adjust * adjust, axis=0)) / width
    rstd = lax.rsqrt(variance + 1e-06)
    adjust = jnp.concatenate([stat_mine[:, 0], stat_other[:, 0]]) - mean
    scale = 1.0 / (jnp.sqrt(F32(width)) * prev_scale)
    index_row = lax.broadcasted_iota(jnp.int32, (own, own), 0)
    index_col = lax.broadcasted_iota(jnp.int32, (own, own), 1)
    table = parity_sign(index_row & index_col).astype(BF)

    prev_parts = jnp.stack(split3(mean_prev.reshape(blocks, own)), axis=1)
    prev_parts = jnp.pad(prev_parts, ((0, 0), (0, 13), (0, 0))).astype(BF)
    features, basis, sums = pl.pallas_call(
        feature_kernel,
        out_shape=(
            jax.ShapeDtypeStruct((blocks, rows, own), BF),
            jax.ShapeDtypeStruct((rows, own), BF),
            jax.ShapeDtypeStruct((blocks, 1, own), F32),
        ),
        in_specs=[smem] + [vmem] * 8,
        out_specs=(vmem,) * 3,
        compiler_params=pltpu.CompilerParams(vmem_limit_bytes=16 << 20),
        cost_estimate=pl.CostEstimate(flops=2 * rows * width * own, bytes_accessed=12 << 20, transcendentals=0),
    )(
        position,
        mine,
        other,
        adjust.T,
        rstd[:, None],
        final_gain.reshape(blocks, 1, own),
        prev_parts,
        rotation,
        (2 * signs - 1).astype(BF)[None, :],
    )
    lines = lax.all_to_all(basis.reshape(blocks, rows // blocks, own), TN, 0, 0, tiled=True)
    moment = pl.pallas_call(
        moment_kernel,
        out_shape=jax.ShapeDtypeStruct((chunks, own, part), BF),
        in_specs=[smem, vmem, vmem],
        out_specs=vmem,
        compiler_params=pltpu.CompilerParams(vmem_limit_bytes=12 << 20),
        cost_estimate=pl.CostEstimate(flops=2 * rows * width * own, bytes_accessed=6 << 20, transcendentals=0),
    )(position, features, sums)
    within = lax.psum_scatter(moment, "z", scatter_dimension=0, tiled=True)

    lines = pl.pallas_call(
        hadamard_kernel,
        out_shape=jax.ShapeDtypeStruct(lines.shape, BF),
        in_specs=[smem, vmem, vmem],
        out_specs=vmem,
        compiler_params=pltpu.CompilerParams(vmem_limit_bytes=12 << 20),
    )(scale, lines, table)
    target = lax.all_to_all(lines, TN, 0, 0, tiled=True).reshape(rows, own)

    sent = pl.pallas_call(
        grad_kernel,
        out_shape=jax.ShapeDtypeStruct((chunks, 2 * depth + 16, part), BF),
        in_specs=[smem] + [vmem] * 5,
        out_specs=vmem,
        compiler_params=pltpu.CompilerParams(vmem_limit_bytes=12 << 20),
    )(position, target, predicted, token_weight, normed, sums)
    taken = lax.all_to_all(sent, DP, 0, 0, tiled=True)

    grad_own = jnp.sum(taken[:, : 2 * depth, :].astype(F32), axis=0).astype(BF)
    within = lax.psum_scatter(within, "yh", scatter_dimension=0, tiled=True)
    grads = lax.cond(
        positive,
        lambda block: broadcast_gather(block, DP),
        lambda block: lax.all_gather(block, DP, axis=0, tiled=False),
        grad_own,
    )
    grad_head = pl.pallas_call(
        place_kernel,
        out_shape=jax.ShapeDtypeStruct((chunks * depth, own), F32),
        in_specs=[vmem],
        out_specs=vmem,
    )(grads)

    tail = taken[:, 2 * depth :, :].astype(F32)
    sums_t = tail[:, 0:6].reshape(chunks, 2, 3, part).sum(2).reshape(chunks, own)
    loss = tail[:, 6:12].reshape(chunks, 2, 3, part).sum((0, 2)).reshape(own)
    sums_d = tail[:, 12:15].sum(1)
    new_mean = jnp.sum(sums_t, axis=0) / all_tokens
    mean_d = jnp.sum(sums_d, axis=0) / all_tokens
    off_t = sums_t / rows - new_mean
    off_d = sums_d / rows - mean_d
    between = lax.dot_general(
        off_t, off_d, (((0,), (0,)), ((), ())), precision=lax.Precision.HIGHEST, preferred_element_type=F32
    )
    new_cov = (within.reshape(own, part).astype(F32) + between * rows) / all_tokens
    return (new_cov, new_mean, grad_head, loss / image_count)


def solution(mesh):
    z, y, x = 8, 4, 4
    if mesh.devices.size != 512:
        z, y, x = 2, mesh.shape["dp"] // 2, mesh.shape["tensor"] // 4
    inner = Mesh(mesh.devices.reshape(z, y, x, 2, 2), DP + TN)
    return jax.shard_map(
        body,
        mesh=inner,
        in_specs=(
            P(DP, TN),
            P(TN, DP),
            P(),
            P(),
            P(None, TN),
            P(TN),
            P(),
            P(DP, None),
            P(None, TN),
            P(),
        ),
        out_specs=(P(TN, DP), P(TN), P(None, TN), P(TN)),
        check_vma=False,
    )
```

```python
import jax
import jax.numpy as jnp
from jax import lax
from jax.experimental import pallas as pl
from jax.experimental.pallas import tpu as pltpu
from jax.sharding import Mesh
from jax.sharding import PartitionSpec as P

DP = ("z", "yh")
TN = ("x", "yl", "c")
IMAGE_SHARE = 128
BF = jnp.bfloat16
F32 = jnp.float32


def hold(value):
    return lax.reduce_precision(value, 8, 7)


def split3(value):
    high = hold(value)
    rest = value - high
    mid = hold(rest)
    return high, mid, rest - mid


def broadcast_gather(block, axes):
    count = lax.axis_size(axes)
    return lax.all_to_all(jnp.broadcast_to(block[None], (count,) + block.shape), axes, 0, 0, tiled=True)


def shift(block, axis, step):
    count = lax.axis_size(axis)
    return lax.ppermute(block, axis, [(i, (i + step) % count) for i in range(count)])


def tensor_gather(block):
    mine = broadcast_gather(block, TN[:2])
    return mine, lax.ppermute(mine, "c", [(0, 1), (1, 0)])


def tensor_gather_twice(block):
    other = lax.ppermute(block, "c", [(0, 1), (1, 0)])
    return broadcast_gather(block, TN[:2]), broadcast_gather(other, TN[:2])


def parity_sign(value):
    count = jnp.zeros_like(value)
    for place in range(16):
        count = count + (value >> place & 1)
    return 1 - 2 * (count % 2)


def layer_norm(values):
    centred = values - jnp.mean(values, axis=-1, keepdims=True)
    spread = jnp.mean(centred * centred, axis=-1, keepdims=True)
    return centred * lax.rsqrt(spread + 1e-06)


def fetch(copies):
    for copy in copies:
        copy.start()
    return copies


def project_kernel(pos_ref, mine_hbm, other_hbm, w_hbm, out_ref, stat_ref, x_ref, w_ref, x_sem, w_sem):
    count, own = x_ref.shape[0], x_ref.shape[2]
    core = lax.rem(pos_ref[0], 2)
    order = [(mine_hbm, q, 2 * q + core) for q in range(count // 2)]
    order += [(other_hbm, q, 2 * q + 1 - core) for q in range(count // 2)]
    x_copies, w_copies = [], []
    for j, (source, q, b) in enumerate(order):
        x_copies += fetch([pltpu.make_async_copy(source.at[q], x_ref.at[j], x_sem.at[j])])
        w_copies += fetch([pltpu.make_async_copy(w_hbm.at[b], w_ref.at[j], w_sem.at[j])])
    total = jnp.zeros(out_ref.shape, F32)
    for j in range(count):
        x_copies[j].wait()
        w_copies[j].wait()
        total += jnp.dot(x_ref[j], w_ref[j], preferred_element_type=F32)
    mean = jnp.sum(total, axis=1, keepdims=True) * (1.0 / own)
    centred = total - mean
    out_ref[...] = centred.astype(BF)
    spread = jnp.sum(centred * centred, axis=1, keepdims=True)
    lane = lax.broadcasted_iota(jnp.int32, stat_ref.shape, 1)
    stat_ref[...] = jnp.where(lane == 0, mean, spread)


def feature_kernel(
    pos_ref, mine_ref, other_ref, adj_ref, rstd_ref, gain_ref, prev_ref, rot_ref, sign_ref,
    f_ref, basis_ref, sums_ref,
):
    blocks, rows, own = f_ref.shape
    core = lax.rem(pos_ref[0], 2)
    rstd = rstd_ref[...]
    total = jnp.zeros((rows, own), F32)
    offset = jnp.zeros((16, own), F32)
    for j in range(blocks):
        source, q, side = (mine_ref, j, core) if j < blocks // 2 else (other_ref, j - blocks // 2, 1 - core)
        b = 2 * q + side
        value = (source[q, :rows, :].astype(F32) + adj_ref[:, j : j + 1]) * rstd * gain_ref[b]
        feature = value.astype(BF)
        f_ref[b] = feature
        sums_ref[b] = jnp.sum(feature.astype(F32), axis=0, keepdims=True)
        turn = rot_ref[pl.ds(pl.multiple_of(b * own, own), own), :]
        total += jnp.dot(feature, turn, preferred_element_type=F32)
        offset += jnp.dot(prev_ref[b], turn, preferred_element_type=F32)
    total -= jnp.sum(offset, axis=0, keepdims=True)
    basis_ref[...] = total.astype(BF) * sign_ref[...]


def moment_kernel(pos_ref, f_ref, sums_ref, out_ref):
    blocks, rows, own = f_ref.shape
    part = out_ref.shape[2]
    own_t = f_ref[pos_ref[0]].astype(F32).T
    own_col = jnp.sum(own_t, axis=1, keepdims=True)
    own_t = own_t.astype(BF)
    for b in range(blocks):
        block = jnp.dot(own_t, f_ref[b], preferred_element_type=F32) - own_col * (sums_ref[b] * (1.0 / rows))
        block = block.astype(BF)
        for h in range(2):
            out_ref[2 * b + h] = block[:, h * part : (h + 1) * part]


def hadamard_kernel(scale_ref, basis_ref, table_ref, out_ref):
    blocks, few, own = basis_ref.shape
    flat = basis_ref[...].reshape(blocks * few, own)
    mixed = jnp.dot(flat, table_ref[...], preferred_element_type=F32) * scale_ref[0]
    parts = [mixed[b * few : (b + 1) * few] for b in range(blocks)]
    step = 1
    while step < blocks:
        parts = [
            parts[b - step] - parts[b] if b & step else parts[b] + parts[b + step] for b in range(blocks)
        ]
        step *= 2
    for b in range(blocks):
        out_ref[b] = parts[b].astype(BF)


def grad_kernel(pos_ref, target_ref, pred_ref, w_ref, normed_ref, sums_ref, out_ref):
    chunks, _, part = out_ref.shape
    depth = normed_ref.shape[1] // chunks
    residual = pred_ref[...] - target_ref[...].astype(F32)
    weighted = residual * w_ref[...]
    loss = jnp.sum(weighted * residual, axis=0, keepdims=True)
    grad = lax.dot_general(
        normed_ref[...], weighted.astype(BF), (((0,), (0,)), ((), ())), preferred_element_type=F32
    ).astype(BF)
    row = lax.broadcasted_iota(jnp.int32, (16, part), 0)

    def parts(value):
        high = value.astype(BF).astype(F32)
        rest = value - high
        mid = rest.astype(BF).astype(F32)
        return [high, mid, rest - mid]

    own_row = sums_ref[pos_ref[0]]
    fixed = []
    for h in range(2):
        fixed += parts(own_row[:, h * part : (h + 1) * part])
    for h in range(2):
        fixed += parts(loss[:, h * part : (h + 1) * part])
    for d in range(chunks):
        for h in range(2):
            out_ref[d, h * depth : (h + 1) * depth, :] = grad[
                d * depth : (d + 1) * depth, h * part : (h + 1) * part
            ]
        tile = jnp.zeros((16, part), F32)
        here = sums_ref[d // 2][:, (d % 2) * part : (d % 2 + 1) * part]
        for i, piece in enumerate(fixed + parts(here)):
            tile = jnp.where(row == i, piece, tile)
        out_ref[d, 2 * depth :, :] = tile.astype(BF)


def place_kernel(in_ref, out_ref):
    chunks, tall, part = in_ref.shape
    depth = tall // 2
    for d in range(chunks):
        for h in range(2):
            out_ref[d * depth : (d + 1) * depth, h * part : (h + 1) * part] = in_ref[
                d, h * depth : (h + 1) * depth, :
            ].astype(F32)


def body(
    teacher_in,
    out_proj,
    final_gain,
    mean_prev,
    rotation,
    signs,
    prev_scale,
    student_in,
    head_weight,
    image_ids,
):
    rows, own = teacher_in.shape
    part = out_proj.shape[1]
    width = final_gain.shape[0]
    blocks = width // own
    chunks = width // part
    depth = student_in.shape[1] // chunks
    all_tokens = image_ids.shape[0]
    image_count = all_tokens // IMAGE_SHARE
    dpos = lax.axis_index(DP)
    tpos = lax.axis_index(TN)

    side = dpos % 2
    halves = out_proj.reshape(2, part, part)
    got = []
    for k in range(2):
        send = lax.dynamic_index_in_dim(halves, (side + k) % 2, 0, keepdims=False)
        route = []
        for d in range(chunks):
            for t in range(blocks):
                route.append((d * blocks + t, (2 * t + (d % 2 ^ k)) * blocks + d // 2))
        got.append(lax.ppermute(send, DP + TN, route))
    strip = jnp.where(
        side == 0, jnp.concatenate(got, axis=1), jnp.concatenate(got[::-1], axis=1)
    )
    near = broadcast_gather(strip, "yh")
    proj = lax.all_gather(near.reshape(-1, own), "z", axis=0, tiled=True)
    teacher, _ = lax.optimization_barrier((teacher_in, near))
    positive = prev_scale[0] > 0.0
    teacher = lax.cond(positive, tensor_gather, tensor_gather_twice, teacher)

    normed = layer_norm(student_in.astype(F32)).astype(BF)
    predicted = jnp.dot(normed, head_weight, preferred_element_type=F32)
    image_nums = jnp.arange(image_count, dtype=jnp.int32)
    counts = jnp.sum((image_ids[None, :] == image_nums[:, None]).astype(F32), axis=1)
    own_ids = lax.dynamic_slice_in_dim(image_ids, dpos * rows, rows, 0)
    token_counts = jnp.sum(
        jnp.where(own_ids[:, None] == image_nums[None, :], counts[None, :], 0.0), axis=1, keepdims=True
    )
    token_weight = 1.0 / token_counts

    smem, vmem = pl.BlockSpec(memory_space=pltpu.SMEM), pl.BlockSpec(memory_space=pltpu.VMEM)
    anywhere = pl.BlockSpec(memory_space=pl.ANY)
    position = tpos.reshape(1)
    raw, stat = pl.pallas_call(
        project_kernel,
        out_shape=(jax.ShapeDtypeStruct((rows, own), BF), jax.ShapeDtypeStruct((rows, 2), F32)),
        in_specs=[smem] + [anywhere] * 3,
        out_specs=(vmem, vmem),
        scratch_shapes=[
            pltpu.VMEM((blocks, rows, own), BF),
            pltpu.VMEM((blocks, own, own), BF),
            pltpu.SemaphoreType.DMA((blocks,)),
            pltpu.SemaphoreType.DMA((blocks,)),
        ],
        compiler_params=pltpu.CompilerParams(vmem_limit_bytes=52 << 20),
        cost_estimate=pl.CostEstimate(flops=2 * rows * width * own, bytes_accessed=8 << 20, transcendentals=0),
    )(position, *teacher, proj.reshape(blocks, own, own))
    pieces = jnp.stack(split3(stat.T)).reshape(6 * rows // own, own).astype(BF)
    spare = -pieces.shape[0] % 16
    packed = jnp.concatenate([raw, pieces, jnp.zeros((spare, own), BF)])
    mine, other = tensor_gather(packed)
    first = tpos % 2 == 0

    def unpack(block):
        tail = block[:, rows : rows + pieces.shape[0], :].astype(F32)
        return tail.reshape(blocks // 2, 3, 2, rows).sum(1)

    stat_mine, stat_other = unpack(mine), unpack(other)
    stats = jnp.stack(
        [jnp.where(first, stat_mine, stat_other), jnp.where(first, stat_other, stat_mine)], axis=1
    ).reshape(blocks, 2, rows)
    mean = jnp.mean(stats[:, 0], axis=0)
    adjust = stats[:, 0] - mean
    variance = (jnp.sum(stats[:, 1], axis=0) + own * jnp.sum(adjust * adjust, axis=0)) / width
    rstd = lax.rsqrt(variance + 1e-06)
    adjust = jnp.concatenate([stat_mine[:, 0], stat_other[:, 0]]) - mean
    scale = 1.0 / (jnp.sqrt(F32(width)) * prev_scale)
    index_row = lax.broadcasted_iota(jnp.int32, (own, own), 0)
    index_col = lax.broadcasted_iota(jnp.int32, (own, own), 1)
    table = parity_sign(index_row & index_col).astype(BF)

    prev_parts = jnp.stack(split3(mean_prev.reshape(blocks, own)), axis=1)
    prev_parts = jnp.pad(prev_parts, ((0, 0), (0, 13), (0, 0))).astype(BF)
    features, basis, sums = pl.pallas_call(
        feature_kernel,
        out_shape=(
            jax.ShapeDtypeStruct((blocks, rows, own), BF),
            jax.ShapeDtypeStruct((rows, own), BF),
            jax.ShapeDtypeStruct((blocks, 1, own), F32),
        ),
        in_specs=[smem] + [vmem] * 8,
        out_specs=(vmem,) * 3,
        compiler_params=pltpu.CompilerParams(vmem_limit_bytes=16 << 20),
        cost_estimate=pl.CostEstimate(flops=2 * rows * width * own, bytes_accessed=12 << 20, transcendentals=0),
    )(
        position,
        mine,
        other,
        adjust.T,
        rstd[:, None],
        final_gain.reshape(blocks, 1, own),
        prev_parts,
        rotation,
        (2 * signs - 1).astype(BF)[None, :],
    )
    lines = lax.all_to_all(basis.reshape(blocks, rows // blocks, own), TN, 0, 0, tiled=True)
    moment = pl.pallas_call(
        moment_kernel,
        out_shape=jax.ShapeDtypeStruct((chunks, own, part), BF),
        in_specs=[smem, vmem, vmem],
        out_specs=vmem,
        compiler_params=pltpu.CompilerParams(vmem_limit_bytes=12 << 20),
        cost_estimate=pl.CostEstimate(flops=2 * rows * width * own, bytes_accessed=6 << 20, transcendentals=0),
    )(position, features, sums)
    within = lax.psum_scatter(moment, "z", scatter_dimension=0, tiled=True)

    lines = pl.pallas_call(
        hadamard_kernel,
        out_shape=jax.ShapeDtypeStruct(lines.shape, BF),
        in_specs=[smem, vmem, vmem],
        out_specs=vmem,
        compiler_params=pltpu.CompilerParams(vmem_limit_bytes=12 << 20),
    )(scale, lines, table)
    target = lax.all_to_all(lines, TN, 0, 0, tiled=True).reshape(rows, own)

    sent = pl.pallas_call(
        grad_kernel,
        out_shape=jax.ShapeDtypeStruct((chunks, 2 * depth + 16, part), BF),
        in_specs=[smem] + [vmem] * 5,
        out_specs=vmem,
        compiler_params=pltpu.CompilerParams(vmem_limit_bytes=12 << 20),
    )(position, target, predicted, token_weight, normed, sums)
    taken = lax.all_to_all(sent, DP, 0, 0, tiled=True)

    grad_own = jnp.sum(taken[:, : 2 * depth, :].astype(F32), axis=0).astype(BF)
    within = lax.psum_scatter(within, "yh", scatter_dimension=0, tiled=True)
    grads = lax.cond(
        positive,
        lambda block: broadcast_gather(block, DP),
        lambda block: lax.all_gather(block, DP, axis=0, tiled=False),
        grad_own,
    )
    grad_head = pl.pallas_call(
        place_kernel,
        out_shape=jax.ShapeDtypeStruct((chunks * depth, own), F32),
        in_specs=[vmem],
        out_specs=vmem,
    )(grads)

    tail = taken[:, 2 * depth :, :].astype(F32)
    sums_t = tail[:, 0:6].reshape(chunks, 2, 3, part).sum(2).reshape(chunks, own)
    loss = tail[:, 6:12].reshape(chunks, 2, 3, part).sum((0, 2)).reshape(own)
    sums_d = tail[:, 12:15].sum(1)
    new_mean = jnp.sum(sums_t, axis=0) / all_tokens
    mean_d = jnp.sum(sums_d, axis=0) / all_tokens
    off_t = sums_t / rows - new_mean
    off_d = sums_d / rows - mean_d
    between = lax.dot_general(
        off_t, off_d, (((0,), (0,)), ((), ())), precision=lax.Precision.HIGHEST, preferred_element_type=F32
    )
    new_cov = (within.reshape(own, part).astype(F32) + between * rows) / all_tokens
    return (new_cov, new_mean, grad_head, loss / image_count)


def solution(mesh):
    z, y, x = 8, 4, 4
    if mesh.devices.size != 512:
        z, y, x = 2, mesh.shape["dp"] // 2, mesh.shape["tensor"] // 4
    inner = Mesh(mesh.devices.reshape(z, y, x, 2, 2), DP + TN)
    return jax.shard_map(
        body,
        mesh=inner,
        in_specs=(
            P(DP, TN),
            P(TN, DP),
            P(),
            P(),
            P(None, TN),
            P(TN),
            P(),
            P(DP, None),
            P(None, TN),
            P(),
        ),
        out_specs=(P(TN, DP), P(TN), P(None, TN), P(TN)),
        check_vma=False,
    )
```
